32 devices in a mesh: energy: 8 (over z, y), seg: 4 (over x, core).
Axes of the slice: x: 2, y: 2, z: 4, core: 2. Of those that a mesh axis runs over, the one named last changes fastest.
Arguments:
- lesser: float32 [32, 8, 2, 256, 256], P('energy', 'seg'), may hold values from -6 to 6
- greater: float32 [32, 8, 2, 256, 256], P('energy', 'seg'), may hold values from -6 to 6
- coupling_low: float32 [32, 8, 2, 256, 256], P('energy', 'seg'), may hold values from -0.125 to 0.125
- coupling_up: float32 [32, 8, 2, 256, 256], P('energy', 'seg'), may hold values from -0.125 to 0.125
Outputs:
- polarization: float32 [32, 8, 2, 256, 256], P('energy', 'seg')
- lesser_full: float32 [32, 8, 2, 256, 256], P('energy', 'seg')
The draws below stay inside these ranges and needn't reach their ends.
All inputs are finite; a program needn't handle non-finite values.
Results may differ from the reference program's by a relative error of at most 0.0001.
Values sent between devices are 32-bit elements; how exact they have to be, the bound alone decides.
A program may use at most 128 MiB of HBM per device.

```python
import math
import jax
import jax.numpy as jnp
from jax import lax

BLOCK = 256
ENERGIES = 32
SEGMENTS = 8


def block_scale(own_key, dims, cuts, smallest, largest):
    def one(axis_at, blocks):
        heights = jax.random.uniform(jax.random.fold_in(jax.random.fold_in(own_key, 6), axis_at), (blocks,), jnp.float32, smallest / len(cuts), largest / len(cuts))
        return jnp.repeat(jnp.exp(heights), dims[axis_at] // blocks).reshape((-1,) + (1,) * (len(dims) - axis_at - 1))

    loudness = one(*cuts[0])
    for cut in cuts[1:]:
        loudness = loudness * one(*cut)
    return loudness


def noise(key, shape, width, limit, pieces=(), kind=jnp.bfloat16):
    loudness = block_scale(key, shape, pieces, -0.22, 0.18) if pieces else 1.0
    drawn = jax.random.normal(key, shape, jnp.float32) * width * loudness
    return jnp.minimum(jnp.maximum(drawn, -limit), limit).astype(kind)


def setup_inputs(seed: int = 0) -> dict:
    splits = jax.random.split(jax.random.key(seed), 5)
    lesser = noise(splits[0], (ENERGIES, SEGMENTS, 2, BLOCK, BLOCK), 1.0, 6.0, ((0, 8), (1, 4)), jnp.float32)
    greater = noise(splits[1], (ENERGIES, SEGMENTS, 2, BLOCK, BLOCK), 1.0, 6.0, ((0, 8), (1, 4)), jnp.float32)
    coupling_low = noise(splits[2], (ENERGIES, SEGMENTS, 2, BLOCK, BLOCK), (8 * BLOCK) ** -0.5, 0.125, ((0, 8), (1, 4)), jnp.float32)
    coupling_up = noise(splits[3], (ENERGIES, SEGMENTS, 2, BLOCK, BLOCK), (8 * BLOCK) ** -0.5, 0.125, ((0, 8), (1, 4)), jnp.float32)
    return {"lesser": lesser, "greater": greater, "coupling_low": coupling_low, "coupling_up": coupling_up}


def complex_product(former, latter):

    def multiply(one_part, two_part):
        return jnp.einsum('eij,ejk->eik', one_part, two_part, precision=lax.Precision.HIGHEST)
    real_part = multiply(former[:, 0], latter[:, 0]) - multiply(former[:, 1], latter[:, 1])
    imag_part = multiply(former[:, 0], latter[:, 1]) + multiply(former[:, 1], latter[:, 0])
    return jnp.stack([real_part, imag_part], axis=1)

def correlate_segment(pair_rows):
    lesser_seg, greater_seg = pair_rows
    energies_all = lesser_seg.shape[0]
    lesser_cplx = lax.complex(lesser_seg[:, 0], lesser_seg[:, 1])
    greater_cplx = lax.complex(greater_seg[:, 0], greater_seg[:, 1])
    lesser_freq = jnp.fft.fft(lesser_cplx, n=2 * energies_all, axis=0)
    greater_freq = jnp.fft.fft(greater_cplx, n=2 * energies_all, axis=0)
    joined = jnp.fft.ifft(lesser_freq * jnp.conj(greater_freq), axis=0)[:energies_all]
    joined = joined * (1.0 / math.sqrt(energies_all))
    return jnp.stack([jnp.real(joined), jnp.imag(joined)], axis=1).astype(lesser_seg.dtype)

def reference(lesser, greater, coupling_low, coupling_up):
    energies_all = lesser.shape[0]
    count = lesser.shape[1]
    block_size = lesser.shape[-1]
    eye_block = jnp.eye(block_size, dtype=lesser.dtype)
    identity = jnp.broadcast_to(jnp.stack([eye_block, jnp.zeros_like(eye_block)]), (energies_all, 2, block_size, block_size))
    corner_low = coupling_low + identity[:, None]
    corner_up = coupling_up + identity[:, None]
    lefts = [identity]
    for segment in range(1, count):
        lefts.append(complex_product(corner_low[:, segment - 1], lefts[-1]))
    rights = [identity]
    for segment in range(count - 2, -1, -1):
        rights.insert(0, complex_product(corner_up[:, segment + 1], rights[0]))
    transfer = jnp.stack([complex_product(lefts[segment], rights[segment]) for segment in range(count)], axis=1)
    lesser_full = lesser + transfer
    greater_full = greater + jnp.stack([transfer[:, :, 0], -transfer[:, :, 1]], axis=2)
    polar = lax.map(correlate_segment, (jnp.swapaxes(lesser_full, 0, 1), jnp.swapaxes(greater_full, 0, 1)))
    return (jnp.swapaxes(polar, 0, 1), lesser_full)
```

```python
import functools
import math

import jax
import jax.numpy as jnp
from jax import lax
from jax.experimental import pallas as pl
from jax.experimental.pallas import tpu as pltpu
from jax.sharding import PartitionSpec as P

MESH = pl.DeviceIdType.MESH
ROWS = 16
LAG = 4
WINDOW = 3


def complex_product(former, latter):

    def multiply(one_part, two_part):
        return jnp.einsum("...ij,...jk->...ik", one_part, two_part, precision=lax.Precision.HIGH)

    real_part = multiply(former[..., 0, :, :], latter[..., 0, :, :]) - multiply(
        former[..., 1, :, :], latter[..., 1, :, :]
    )
    imag_part = multiply(former[..., 0, :, :], latter[..., 1, :, :]) + multiply(
        former[..., 1, :, :], latter[..., 0, :, :]
    )
    return jnp.stack([real_part, imag_part], axis=-3)


def swap_pairs(part):
    return lax.ppermute(part, "seg", [(0, 1), (1, 0), (2, 3), (3, 2)])


def chain(coupling_low, coupling_up):
    place = lax.axis_index("seg")
    even = place % 2 == 0
    outer = (place == 0) | (place == 3)
    energies = coupling_low.shape[0]
    block_size = coupling_low.shape[-1]
    eye_block = jnp.eye(block_size, dtype=jnp.float32)
    identity = jnp.broadcast_to(
        jnp.stack([eye_block, jnp.zeros_like(eye_block)]), (energies, 2, block_size, block_size)
    )
    low = [coupling_low[:, s] + identity for s in range(2)]
    up = [coupling_up[:, s] + identity for s in range(2)]
    low_total = complex_product(low[1], low[0])
    up_total = complex_product(up[0], up[1])
    near = swap_pairs(jnp.where(even, low_total, up_total))
    pair = complex_product(jnp.where(even, up_total, low_total), near)
    half = energies // 2
    to_outer = lax.ppermute(pair[:half], "seg", [(1, 3), (2, 0)])
    to_inner = lax.ppermute(pair[half:], "seg", [(1, 2), (2, 1)])
    mine = jnp.where(outer, to_outer, to_inner)
    other = swap_pairs(mine)
    far = jnp.concatenate([jnp.where(outer, mine, other), jnp.where(outer, other, mine)], axis=0)
    both = complex_product(near, far)
    left = jnp.where(
        place == 0, identity, jnp.where(place == 1, near, jnp.where(place == 2, far, both))
    )
    right = jnp.where(
        place == 0, both, jnp.where(place == 1, far, jnp.where(place == 2, near, identity))
    )
    first = complex_product(left, complex_product(up[1], right))
    second = complex_product(complex_product(low[0], left), right)
    return jnp.stack([first, second], axis=1)


def block_terms(lesser_ref, greater_ref, rows, columns, later):
    size = lesser_ref.shape[0]
    l_re, l_im = lesser_ref[:, 0, rows, columns], lesser_ref[:, 1, rows, columns]
    g_re, g_im = greater_ref[:, 0, rows, columns], greater_ref[:, 1, rows, columns]
    terms = []
    for shift in range(size):
        if later and shift == 0:
            terms.append(None)
            continue
        if later:
            here, there = slice(0, shift), slice(size - shift, size)
        else:
            here, there = slice(shift, size), slice(0, size - shift)
        real_part = l_re[here] * g_re[there] + l_im[here] * g_im[there]
        imag_part = l_im[here] * g_re[there] - l_re[here] * g_im[there]
        terms.append((jnp.sum(real_part, axis=0), jnp.sum(imag_part, axis=0)))
    return terms


def correlate_block(out_ref, pairs, rows, columns, scale):
    total = None
    for lesser_ref, greater_ref, later in pairs:
        terms = block_terms(lesser_ref, greater_ref, rows, columns, later)
        if total is None:
            total = terms
        else:
            total = [
                old if new is None else (old[0] + new[0], old[1] + new[1])
                for old, new in zip(total, terms)
            ]
    for shift, (real_part, imag_part) in enumerate(total):
        out_ref[shift, 0, rows, columns] = real_part * scale
        out_ref[shift, 1, rows, columns] = imag_part * scale


def exchange_kernel(
    scale,
    lesser,
    greater,
    out,
    l_own,
    g_own,
    g_one,
    g_two,
    in_a,
    in_b,
    part,
    own_sem,
    y_send,
    y_recv,
    f_send,
    f_recv,
    o_send,
    o_recv,
    o_own,
):
    chunks, block, _, rows, width = l_own.shape
    share = block // 2
    per_segment = chunks // lesser.shape[1]
    half_rows = lesser.shape[3] // 2
    place = lax.axis_index("energy")
    line = place // 2
    side = place % 2
    partner = place + 1 - 2 * side

    def region(ref, chunk, half):
        start = pl.multiple_of(half * half_rows + (chunk % per_segment) * rows, rows)
        return ref.at[:, chunk // per_segment, :, pl.ds(start, rows), :]

    def remote(source, target, send, recv, device):
        return pltpu.make_async_remote_copy(
            src_ref=source,
            dst_ref=target,
            send_sem=send,
            recv_sem=recv,
            device_id={"energy": device},
            device_id_type=MESH,
        )

    def own_copy(which, chunk):
        source, target = ((lesser, l_own), (greater, g_own))[which]
        return pltpu.make_async_copy(
            region(source, chunk, side),
            target.at[chunk, pl.ds(side * share, share)],
            own_sem.at[which, chunk],
        )

    def side_copy(which, chunk):
        source, target = ((lesser, l_own), (greater, g_own))[which]
        return remote(
            region(source, chunk, 1 - side),
            target.at[chunk, pl.ds(side * share, share)],
            y_send.at[which, chunk],
            y_recv.at[which, chunk],
            partner,
        )

    def issue(chunk):
        for which in (1, 0):
            side_copy(which, chunk).start()
            own_copy(which, chunk).start()

    def ready(which, chunk):
        own_copy(which, chunk).wait()
        side_copy(which, chunk).wait_recv()

    def along(source, target, send, recv, chunk, device):
        return remote(source, target, f_send.at[send, chunk], f_recv.at[recv, chunk], device)

    def arrived(recv, chunk):
        target = (g_one, g_two, in_a, in_b)[recv].at[chunk]
        along(target, target, recv, recv, chunk, partner).wait_recv()

    def result_copy(result, chunk):
        return remote(
            result.at[pl.ds((1 - side) * share, share)],
            region(out, chunk, side),
            o_send.at[chunk],
            o_recv.at[chunk],
            partner,
        )

    def result_own(result, chunk):
        return pltpu.make_async_copy(
            result.at[pl.ds(side * share, share)], region(out, chunk, side), o_own.at[chunk]
        )

    def finish(result, chunk):
        result_copy(result, chunk).start()
        result_own(result, chunk).start()

    def tiles(body):
        columns = width // 128

        def one(index, carry):
            row = pl.multiple_of((index // columns) * 8, 8)
            column = pl.multiple_of((index % columns) * 128, 128)
            body(pl.ds(row, 8), pl.ds(column, 128))
            return carry

        lax.fori_loop(0, (rows // 8) * columns, one, 0)

    def correlate(chunk, *blocks):
        def body(row, column):
            for index, pairs in blocks:
                correlate_block(part.at[chunk, index], pairs, row, column, scale)

        tiles(body)

    def add_in(index, source, chunk):
        part[chunk, index] = part[chunk, index] + source[chunk]

    def sends(chunk):
        return (
            (along(g_own.at[chunk], g_one.at[chunk], 0, 0, chunk, place + 2),),
            (
                along(g_own.at[chunk], g_one.at[chunk], 0, 0, chunk, place + 2),
                along(g_one.at[chunk], g_two.at[chunk], 1, 1, chunk, place + 2),
                along(part.at[chunk, 0], in_a.at[chunk], 2, 2, chunk, place - 2),
            ),
            (
                along(part.at[chunk, 0], in_a.at[chunk], 0, 2, chunk, place - 2),
                along(part.at[chunk, 1], in_b.at[chunk], 1, 3, chunk, place - 2),
                along(part.at[chunk, 3], in_a.at[chunk], 2, 2, chunk, place + 2),
            ),
            (
                along(l_own.at[chunk], in_a.at[chunk], 0, 2, chunk, place - 2),
                along(g_own.at[chunk], in_b.at[chunk], 1, 3, chunk, place - 2),
            ),
        )

    def result_of(index, chunk):
        return in_a.at[chunk] if index == 3 else part.at[chunk, index]

    def forward(index, chunk):
        l_here, g_here = l_own.at[chunk], g_own.at[chunk]
        one, two = g_one.at[chunk], g_two.at[chunk]
        l_next, g_next = in_a.at[chunk], in_b.at[chunk]
        moves = sends(chunk)[index]
        if index == 0:
            ready(1, chunk)
            moves[0].start()
            ready(0, chunk)
            correlate(chunk, (0, [(l_here, g_here, False)]))
        elif index == 1:
            ready(1, chunk)
            moves[0].start()
            arrived(0, chunk)
            moves[1].start()
            ready(0, chunk)
            correlate(
                chunk,
                (0, [(l_here, g_here, False), (l_here, one, True)]),
                (1, [(l_here, one, False)]),
            )
        elif index == 2:
            ready(1, chunk)
            ready(0, chunk)
            for recv in (2, 3, 0, 1):
                arrived(recv, chunk)
            correlate(
                chunk,
                (
                    0,
                    [
                        (l_here, g_here, False),
                        (l_next, g_next, False),
                        (l_here, one, True),
                        (l_next, g_here, True),
                    ],
                ),
                (
                    1,
                    [
                        (l_here, one, False),
                        (l_next, g_here, False),
                        (l_here, two, True),
                        (l_next, one, True),
                    ],
                ),
                (2, [(l_here, two, False), (l_next, one, False), (l_next, two, True)]),
                (3, [(l_next, two, False)]),
            )
            for move in moves:
                move.start()
            finish(result_of(2, chunk), chunk)
        else:
            ready(0, chunk)
            moves[0].start()
            ready(1, chunk)
            moves[1].start()

    def back(index, chunk):
        if index == 0:
            arrived(2, chunk)
            add_in(0, in_a, chunk)
        elif index == 1:
            arrived(2, chunk)
            add_in(0, in_a, chunk)
            sends(chunk)[1][2].start()
            arrived(3, chunk)
            add_in(1, in_b, chunk)
        elif index == 3:
            arrived(2, chunk)
        if index != 2:
            finish(result_of(index, chunk), chunk)

    barrier = pltpu.get_barrier_semaphore()

    def greet(device):
        pl.semaphore_signal(barrier, inc=1, device_id={"energy": device}, device_id_type=MESH)

    greet(partner)

    @pl.when(line > 0)
    def _():
        greet(place - 2)

    @pl.when(line < 3)
    def _():
        greet(place + 2)

    inner = (line > 0) & (line < 3)

    @pl.when(inner)
    def _():
        pl.semaphore_wait(barrier, 3)

    @pl.when(jnp.logical_not(inner))
    def _():
        pl.semaphore_wait(barrier, 2)

    def start_one(chunk, carry):
        issue(chunk)
        return carry

    lax.fori_loop(0, min(WINDOW, chunks), start_one, 0)

    def role(index):
        lag = LAG + 2 if index == 0 else LAG

        def step(turn, carry):
            @pl.when(turn + WINDOW < chunks)
            def _():
                issue(turn + WINDOW)

            @pl.when(turn < chunks)
            def _():
                forward(index, turn)

            if index != 2:

                @pl.when(turn >= lag)
                def _():
                    back(index, turn - lag)

            return carry

        lax.fori_loop(0, chunks + (0 if index == 2 else lag), step, 0)

        def settle(chunk, carry):
            for which in (0, 1):
                side_copy(which, chunk).wait_send()
            for move in sends(chunk)[index]:
                move.wait_send()
            result = result_of(index, chunk)
            result_own(result, chunk).wait()
            result_copy(result, chunk).wait()
            return carry

        lax.fori_loop(0, chunks, settle, 0)

    for index in range(4):

        @pl.when(line == index)
        def _(index=index):
            role(index)


def correlate_on_line(lesser_full, greater_full):
    share, segments, _, size, width = lesser_full.shape
    chunks = segments * (size // 2) // ROWS
    block = 2 * share
    energies = share * lax.axis_size("energy")
    buffer = pltpu.VMEM((chunks, block, 2, ROWS, width), jnp.float32)
    dma = pltpu.SemaphoreType.DMA
    elements = segments * size * width
    return pl.pallas_call(
        functools.partial(exchange_kernel, 1.0 / math.sqrt(energies)),
        out_shape=jax.ShapeDtypeStruct(lesser_full.shape, jnp.float32),
        in_specs=[pl.BlockSpec(memory_space=pl.ANY)] * 2,
        out_specs=pl.BlockSpec(memory_space=pl.ANY),
        scratch_shapes=[buffer] * 6
        + [pltpu.VMEM((chunks, 4, block, 2, ROWS, width), jnp.float32)]
        + [dma((2, chunks))] * 3
        + [dma((4, chunks))] * 2
        + [dma((chunks,))] * 3,
        compiler_params=pltpu.CompilerParams(
            collective_id=0, has_side_effects=True, vmem_limit_bytes=56 * 1024 * 1024
        ),
        cost_estimate=pl.CostEstimate(
            flops=elements * 400 * 8, bytes_accessed=elements * share * 24, transcendentals=0
        ),
    )(lesser_full, greater_full)


def correlate_rows(lesser_rows, greater_rows):
    energies = lesser_rows.shape[0]
    l_re, l_im = lesser_rows[:, :, 0], lesser_rows[:, :, 1]
    g_re, g_im = greater_rows[:, :, 0], greater_rows[:, :, 1]
    scale = 1.0 / math.sqrt(energies)

    def one(shift, result):
        held = (jnp.arange(energies) + shift < energies)[:, None, None, None]
        s_re = jnp.where(held, jnp.roll(l_re, -shift, axis=0), 0.0)
        s_im = jnp.where(held, jnp.roll(l_im, -shift, axis=0), 0.0)
        real_part = jnp.sum(s_re * g_re + s_im * g_im, axis=0)
        imag_part = jnp.sum(s_im * g_re - s_re * g_im, axis=0)
        row = jnp.stack([real_part, imag_part], axis=1) * scale
        return lax.dynamic_update_index_in_dim(result, row, shift, 0)

    return lax.fori_loop(0, energies, one, jnp.zeros_like(lesser_rows))


def correlate_all(lesser_full, greater_full):
    rows = [
        lax.all_to_all(array, "energy", split_axis=3, concat_axis=0, tiled=True)
        for array in (lesser_full, greater_full)
    ]
    return lax.all_to_all(
        correlate_rows(*rows), "energy", split_axis=0, concat_axis=3, tiled=True
    )


def on_device(lesser, greater, coupling_low, coupling_up):
    transfer = chain(coupling_low, coupling_up)
    lesser_full = lesser + transfer
    greater_full = jnp.stack(
        [greater[:, :, 0] + transfer[:, :, 0], greater[:, :, 1] - transfer[:, :, 1]], axis=2
    )
    if lax.axis_size("energy") == 8:
        polarization = correlate_on_line(lesser_full, greater_full)
    else:
        polarization = correlate_all(lesser_full, greater_full)
    return (polarization, lesser_full)


def solution(mesh):
    spec = P("energy", "seg", None, None, None)
    return jax.shard_map(
        on_device,
        mesh=mesh,
        in_specs=(spec, spec, spec, spec),
        out_specs=(spec, spec),
        check_vma=False,
    )
```

```python
import functools
import math

import jax
import jax.numpy as jnp
from jax import lax
from jax.experimental import pallas as pl
from jax.experimental.pallas import tpu as pltpu
from jax.sharding import PartitionSpec as P

MESH = pl.DeviceIdType.MESH
ROWS = 16
LAG = 4
WINDOW = 3


LOW, UP, LOW_TOTAL, UP_TOTAL, PAIR, IDENTITY, NEAR, FAR, BOTH, LEFT_ONE, RIGHT_ONE, FIRST, SECOND = (
    0, 2, 4, 5, 6, 7, 8, 9, 10, 11, 12, 13, 14,
)
SLOTS = 15


def halves(value):
    high = value.astype(jnp.bfloat16)
    return high, (value - high.astype(jnp.float32)).astype(jnp.bfloat16)


def off_identity_product(held, target, former, latter, energy):
    f_re, f_im = held[former, energy, 0], held[former, energy, 1]
    l_re, l_im = held[latter, energy, 0], held[latter, energy, 1]
    size = f_re.shape[0]
    f_high, f_low = halves(jnp.concatenate([f_re, f_im], axis=1))
    l_high, l_low = halves(
        jnp.concatenate(
            [jnp.concatenate([l_re, l_im], axis=1), jnp.concatenate([-l_im, l_re], axis=1)], axis=0
        )
    )

    def multiply(one, two):
        return jnp.dot(one, two, preferred_element_type=jnp.float32)

    both = multiply(f_high, l_high) + (multiply(f_high, l_low) + multiply(f_low, l_high))
    held[target, energy, 0] = f_re + l_re + both[:, :size]
    held[target, energy, 1] = f_im + l_im + both[:, size:]


def chain_kernel(
    coupling_low, coupling_up, out, held, in_sem, out_sem, near_send, near_recv, far_send, far_recv, relay_send
):
    energies = out.shape[0]
    place = lax.axis_index("seg")
    odd = place % 2
    neighbour = place + 1 - 2 * odd
    across = (place + 2) % 4
    outer = (place == 0) | (place == 3)

    def load(which, segment, energy):
        source = (coupling_low, coupling_up)[which]
        return pltpu.make_async_copy(
            source.at[energy, segment],
            held.at[2 * which + segment, energy],
            in_sem.at[2 * which + segment, energy],
        )

    def store(segment, energy):
        return pltpu.make_async_copy(
            held.at[FIRST + segment, energy], out.at[energy, segment], out_sem.at[segment, energy]
        )

    def remote(source, target, send, recv, device):
        return pltpu.make_async_remote_copy(
            src_ref=source,
            dst_ref=target,
            send_sem=send,
            recv_sem=recv,
            device_id={"seg": device},
            device_id_type=MESH,
        )

    def near(energy):
        return remote(
            held.at[LOW_TOTAL + odd, energy],
            held.at[NEAR, energy],
            near_send.at[energy],
            near_recv.at[energy],
            neighbour,
        )

    def far(energy):
        return remote(
            held.at[PAIR, energy], held.at[FAR, energy], far_send.at[energy], far_recv.at[energy], across
        )

    def relay(energy):
        return remote(
            held.at[FAR, energy], held.at[FAR, energy], relay_send.at[energy], far_recv.at[energy], neighbour
        )

    multiply = functools.partial(off_identity_product, held)

    def each(body, count=energies):
        def one(energy, carry):
            body(energy)
            return carry

        lax.fori_loop(0, count, one, 0)

    def load_one(energy):
        for which in (0, 1):
            for segment in (0, 1):
                load(which, segment, energy).start()

    each(load_one)
    barrier = pltpu.get_barrier_semaphore()
    for device in (neighbour, across):
        pl.semaphore_signal(barrier, inc=1, device_id={"seg": device}, device_id_type=MESH)
    held[IDENTITY] = jnp.zeros(held.shape[1:], jnp.float32)
    pl.semaphore_wait(barrier, 2)

    def totals(turn):
        @pl.when(turn < energies)
        def _():
            for which in (0, 1):
                for segment in (0, 1):
                    load(which, segment, turn).wait()

            multiply(LOW_TOTAL, LOW + 1, LOW, turn)
            multiply(UP_TOTAL, UP, UP + 1, turn)
            near(turn).start()

        @pl.when(turn >= 1)
        def _():
            energy = turn - 1
            near(energy).wait_recv()
            multiply(PAIR, UP_TOTAL - odd, NEAR, energy)

            @pl.when(jnp.logical_not(outer))
            def _():
                far(energy).start()

    each(totals, energies + 1)

    def finish(energy):
        far(energy).wait_recv()

        @pl.when(outer)
        def _():
            relay(energy).start()
            multiply(BOTH, NEAR, FAR, energy)

        left, right = IDENTITY + place, BOTH - place
        multiply(LEFT_ONE, LOW, left, energy)
        multiply(RIGHT_ONE, UP + 1, right, energy)
        multiply(FIRST, left, RIGHT_ONE, energy)
        store(0, energy).start()
        multiply(SECOND, LEFT_ONE, right, energy)
        store(1, energy).start()

    each(finish)

    def settle(energy):
        near(energy).wait_send()

        @pl.when(outer)
        def _():
            relay(energy).wait_send()

        @pl.when(jnp.logical_not(outer))
        def _():
            far(energy).wait_send()

        for segment in (0, 1):
            store(segment, energy).wait()

    each(settle)


def chain(coupling_low, coupling_up):
    energies, segments, _, size, _ = coupling_low.shape
    assert (lax.axis_size("seg"), segments) == (4, 2)
    dma = pltpu.SemaphoreType.DMA
    return pl.pallas_call(
        chain_kernel,
        out_shape=jax.ShapeDtypeStruct(coupling_low.shape, jnp.float32),
        in_specs=[pl.BlockSpec(memory_space=pl.ANY)] * 2,
        out_specs=pl.BlockSpec(memory_space=pl.ANY),
        scratch_shapes=[
            pltpu.VMEM((SLOTS, energies, 2, size, size), jnp.float32),
            dma((4, energies)),
            dma((2, energies)),
        ]
        + [dma((energies,))] * 5,
        compiler_params=pltpu.CompilerParams(
            collective_id=1, has_side_effects=True, vmem_limit_bytes=56 * 1024 * 1024
        ),
        cost_estimate=pl.CostEstimate(
            flops=energies * 8 * 3 * 8 * size**3,
            bytes_accessed=energies * segments * 24 * size**2,
            transcendentals=0,
        ),
    )(coupling_low, coupling_up)


def block_terms(lesser_ref, greater_ref, rows, columns, later):
    size = lesser_ref.shape[0]
    l_re, l_im = lesser_ref[:, 0, rows, columns], lesser_ref[:, 1, rows, columns]
    g_re, g_im = greater_ref[:, 0, rows, columns], greater_ref[:, 1, rows, columns]
    terms = []
    for shift in range(size):
        if later and shift == 0:
            terms.append(None)
            continue
        if later:
            here, there = slice(0, shift), slice(size - shift, size)
        else:
            here, there = slice(shift, size), slice(0, size - shift)
        real_part = l_re[here] * g_re[there] + l_im[here] * g_im[there]
        imag_part = l_im[here] * g_re[there] - l_re[here] * g_im[there]
        terms.append((jnp.sum(real_part, axis=0), jnp.sum(imag_part, axis=0)))
    return terms


def correlate_block(out_ref, pairs, rows, columns, scale):
    total = None
    for lesser_ref, greater_ref, later in pairs:
        terms = block_terms(lesser_ref, greater_ref, rows, columns, later)
        if total is None:
            total = terms
        else:
            total = [
                old if new is None else (old[0] + new[0], old[1] + new[1])
                for old, new in zip(total, terms)
            ]
    for shift, (real_part, imag_part) in enumerate(total):
        out_ref[shift, 0, rows, columns] = real_part * scale
        out_ref[shift, 1, rows, columns] = imag_part * scale


def exchange_kernel(
    scale,
    lesser,
    greater,
    out,
    l_own,
    g_own,
    g_one,
    g_two,
    in_a,
    in_b,
    part,
    own_sem,
    y_send,
    y_recv,
    f_send,
    f_recv,
    o_send,
    o_recv,
    o_own,
):
    chunks, block, _, rows, width = l_own.shape
    share = block // 2
    per_segment = chunks // lesser.shape[1]
    half_rows = lesser.shape[3] // 2
    place = lax.axis_index("energy")
    line = place // 2
    side = place % 2
    partner = place + 1 - 2 * side

    def region(ref, chunk, half):
        start = pl.multiple_of(half * half_rows + (chunk % per_segment) * rows, rows)
        return ref.at[:, chunk // per_segment, :, pl.ds(start, rows), :]

    def remote(source, target, send, recv, device):
        return pltpu.make_async_remote_copy(
            src_ref=source,
            dst_ref=target,
            send_sem=send,
            recv_sem=recv,
            device_id={"energy": device},
            device_id_type=MESH,
        )

    def own_copy(which, chunk):
        source, target = ((lesser, l_own), (greater, g_own))[which]
        return pltpu.make_async_copy(
            region(source, chunk, side),
            target.at[chunk, pl.ds(side * share, share)],
            own_sem.at[which, chunk],
        )

    def side_copy(which, chunk):
        source, target = ((lesser, l_own), (greater, g_own))[which]
        return remote(
            region(source, chunk, 1 - side),
            target.at[chunk, pl.ds(side * share, share)],
            y_send.at[which, chunk],
            y_recv.at[which, chunk],
            partner,
        )

    def issue(chunk):
        for which in (1, 0):
            side_copy(which, chunk).start()
            own_copy(which, chunk).start()

    def ready(which, chunk):
        own_copy(which, chunk).wait()
        side_copy(which, chunk).wait_recv()

    def along(source, target, send, recv, chunk, device):
        return remote(source, target, f_send.at[send, chunk], f_recv.at[recv, chunk], device)

    def arrived(recv, chunk):
        target = (g_one, g_two, in_a, in_b)[recv].at[chunk]
        along(target, target, recv, recv, chunk, partner).wait_recv()

    def result_copy(result, chunk):
        return remote(
            result.at[pl.ds((1 - side) * share, share)],
            region(out, chunk, side),
            o_send.at[chunk],
            o_recv.at[chunk],
            partner,
        )

    def result_own(result, chunk):
        return pltpu.make_async_copy(
            result.at[pl.ds(side * share, share)], region(out, chunk, side), o_own.at[chunk]
        )

    def finish(result, chunk):
        result_copy(result, chunk).start()
        result_own(result, chunk).start()

    def tiles(body):
        columns = width // 128

        def one(index, carry):
            row = pl.multiple_of((index // columns) * 8, 8)
            column = pl.multiple_of((index % columns) * 128, 128)
            body(pl.ds(row, 8), pl.ds(column, 128))
            return carry

        lax.fori_loop(0, (rows // 8) * columns, one, 0)

    def correlate(chunk, *blocks):
        def body(row, column):
            for index, pairs in blocks:
                correlate_block(part.at[chunk, index], pairs, row, column, scale)

        tiles(body)

    def add_in(index, source, chunk):
        part[chunk, index] = part[chunk, index] + source[chunk]

    def sends(chunk):
        def move(source, target, send, recv, device):
            return lambda: along(source, target, send, recv, chunk, device)

        return (
            (move(g_own.at[chunk], g_one.at[chunk], 0, 0, place + 2),),
            (
                move(g_own.at[chunk], g_one.at[chunk], 0, 0, place + 2),
                move(g_one.at[chunk], g_two.at[chunk], 1, 1, place + 2),
                move(part.at[chunk, 0], in_a.at[chunk], 2, 2, place - 2),
            ),
            (
                move(part.at[chunk, 0], in_a.at[chunk], 0, 2, place - 2),
                move(part.at[chunk, 1], in_b.at[chunk], 1, 3, place - 2),
                move(part.at[chunk, 3], in_a.at[chunk], 2, 2, place + 2),
            ),
            (
                move(l_own.at[chunk], in_a.at[chunk], 0, 2, place - 2),
                move(g_own.at[chunk], in_b.at[chunk], 1, 3, place - 2),
            ),
        )

    def result_of(index, chunk):
        return in_a.at[chunk] if index == 3 else part.at[chunk, index]

    def forward(index, chunk):
        l_here, g_here = l_own.at[chunk], g_own.at[chunk]
        one, two = g_one.at[chunk], g_two.at[chunk]
        l_next, g_next = in_a.at[chunk], in_b.at[chunk]
        moves = sends(chunk)[index]
        if index == 0:
            ready(1, chunk)
            moves[0]().start()
            ready(0, chunk)
            correlate(chunk, (0, [(l_here, g_here, False)]))
        elif index == 1:
            ready(1, chunk)
            moves[0]().start()
            arrived(0, chunk)
            moves[1]().start()
            ready(0, chunk)
            correlate(
                chunk,
                (0, [(l_here, g_here, False), (l_here, one, True)]),
                (1, [(l_here, one, False)]),
            )
        elif index == 2:
            ready(1, chunk)
            ready(0, chunk)
            for recv in (2, 3, 0, 1):
                arrived(recv, chunk)
            correlate(
                chunk,
                (
                    0,
                    [
                        (l_here, g_here, False),
                        (l_next, g_next, False),
                        (l_here, one, True),
                        (l_next, g_here, True),
                    ],
                ),
                (
                    1,
                    [
                        (l_here, one, False),
                        (l_next, g_here, False),
                        (l_here, two, True),
                        (l_next, one, True),
                    ],
                ),
                (2, [(l_here, two, False), (l_next, one, False), (l_next, two, True)]),
                (3, [(l_next, two, False)]),
            )
            for move in moves:
                move().start()
            finish(result_of(2, chunk), chunk)
        else:
            ready(0, chunk)
            moves[0]().start()
            ready(1, chunk)
            moves[1]().start()

    def back(index, chunk):
        if index == 0:
            arrived(2, chunk)
            add_in(0, in_a, chunk)
        elif index == 1:
            arrived(2, chunk)
            add_in(0, in_a, chunk)
            sends(chunk)[1][2]().start()
            arrived(3, chunk)
            add_in(1, in_b, chunk)
        elif index == 3:
            arrived(2, chunk)
        if index != 2:
            finish(result_of(index, chunk), chunk)

    barrier = pltpu.get_barrier_semaphore()

    def greet(device):
        pl.semaphore_signal(barrier, inc=1, device_id={"energy": device}, device_id_type=MESH)

    greet(partner)

    @pl.when(line > 0)
    def _():
        greet(place - 2)

    @pl.when(line < 3)
    def _():
        greet(place + 2)

    inner = (line > 0) & (line < 3)

    @pl.when(inner)
    def _():
        pl.semaphore_wait(barrier, 3)

    @pl.when(jnp.logical_not(inner))
    def _():
        pl.semaphore_wait(barrier, 2)

    def start_one(chunk, carry):
        issue(chunk)
        return carry

    lax.fori_loop(0, min(WINDOW, chunks), start_one, 0)

    def role(index):
        lag = LAG + 2 if index == 0 else LAG

        def step(turn, carry):
            @pl.when(turn + WINDOW < chunks)
            def _():
                issue(turn + WINDOW)

            @pl.when(turn < chunks)
            def _():
                forward(index, turn)

            if index != 2:

                @pl.when(turn >= lag)
                def _():
                    back(index, turn - lag)

            return carry

        lax.fori_loop(0, chunks + (0 if index == 2 else lag), step, 0)

        def settle(chunk, carry):
            for which in (0, 1):
                side_copy(which, chunk).wait_send()
            for move in sends(chunk)[index]:
                move().wait_send()
            result = result_of(index, chunk)
            result_own(result, chunk).wait()
            result_copy(result, chunk).wait()
            return carry

        lax.fori_loop(0, chunks, settle, 0)

    for index in range(4):

        @pl.when(line == index)
        def _(index=index):
            role(index)


def correlate_on_line(lesser_full, greater_full):
    share, segments, _, size, width = lesser_full.shape
    chunks = segments * (size // 2) // ROWS
    block = 2 * share
    energies = share * lax.axis_size("energy")
    buffer = pltpu.VMEM((chunks, block, 2, ROWS, width), jnp.float32)
    dma = pltpu.SemaphoreType.DMA
    elements = segments * size * width
    return pl.pallas_call(
        functools.partial(exchange_kernel, 1.0 / math.sqrt(energies)),
        out_shape=jax.ShapeDtypeStruct(lesser_full.shape, jnp.float32),
        in_specs=[pl.BlockSpec(memory_space=pl.ANY)] * 2,
        out_specs=pl.BlockSpec(memory_space=pl.ANY),
        scratch_shapes=[buffer] * 6
        + [pltpu.VMEM((chunks, 4, block, 2, ROWS, width), jnp.float32)]
        + [dma((2, chunks))] * 3
        + [dma((4, chunks))] * 2
        + [dma((chunks,))] * 3,
        compiler_params=pltpu.CompilerParams(
            collective_id=0, has_side_effects=True, vmem_limit_bytes=56 * 1024 * 1024
        ),
        cost_estimate=pl.CostEstimate(
            flops=elements * 400 * 8, bytes_accessed=elements * share * 24, transcendentals=0
        ),
    )(lesser_full, greater_full)


def correlate_rows(lesser_rows, greater_rows):
    energies = lesser_rows.shape[0]
    l_re, l_im = lesser_rows[:, :, 0], lesser_rows[:, :, 1]
    g_re, g_im = greater_rows[:, :, 0], greater_rows[:, :, 1]
    scale = 1.0 / math.sqrt(energies)

    def one(shift, result):
        held = (jnp.arange(energies) + shift < energies)[:, None, None, None]
        s_re = jnp.where(held, jnp.roll(l_re, -shift, axis=0), 0.0)
        s_im = jnp.where(held, jnp.roll(l_im, -shift, axis=0), 0.0)
        real_part = jnp.sum(s_re * g_re + s_im * g_im, axis=0)
        imag_part = jnp.sum(s_im * g_re - s_re * g_im, axis=0)
        row = jnp.stack([real_part, imag_part], axis=1) * scale
        return lax.dynamic_update_index_in_dim(result, row, shift, 0)

    return lax.fori_loop(0, energies, one, jnp.zeros_like(lesser_rows))


def correlate_all(lesser_full, greater_full):
    rows = [
        lax.all_to_all(array, "energy", split_axis=3, concat_axis=0, tiled=True)
        for array in (lesser_full, greater_full)
    ]
    return lax.all_to_all(
        correlate_rows(*rows), "energy", split_axis=0, concat_axis=3, tiled=True
    )


def on_device(lesser, greater, coupling_low, coupling_up):
    size = lesser.shape[-1]
    unit = jnp.eye(size, dtype=jnp.float32) * jnp.array([1.0, 0.0], jnp.float32)[:, None, None]
    sign = jnp.array([1.0, -1.0], jnp.float32)[:, None, None]
    transfer = chain(coupling_low, coupling_up) + unit
    lesser_full = lesser + transfer
    greater_full = greater + sign * transfer
    if lax.axis_size("energy") == 8:
        polarization = correlate_on_line(lesser_full, greater_full)
    else:
        polarization = correlate_all(lesser_full, greater_full)
    return (polarization, lesser_full)


def solution(mesh):
    spec = P("energy", "seg", None, None, None)
    return jax.shard_map(
        on_device,
        mesh=mesh,
        in_specs=(spec, spec, spec, spec),
        out_specs=(spec, spec),
        check_vma=False,
    )
```

```python
import functools
import math

import jax
import jax.numpy as jnp
from jax import lax
from jax.experimental import pallas as pl
from jax.experimental.pallas import tpu as pltpu
from jax.sharding import PartitionSpec as P

MESH = pl.DeviceIdType.MESH
ROWS = 8
LAG = 6
WINDOW = 4


LOW, UP, LOW_TOTAL, UP_TOTAL, PAIR, IDENTITY, NEAR, FAR, BOTH, LEFT_ONE, RIGHT_ONE, FIRST, SECOND = (
    0, 2, 4, 5, 6, 7, 8, 9, 10, 11, 12, 13, 14,
)
SLOTS = 15


def halves(value):
    high = value.astype(jnp.bfloat16)
    return high, (value - high.astype(jnp.float32)).astype(jnp.bfloat16)


def off_identity_product(held, target, former, latter, energy):
    f_re, f_im = held[former, energy, 0], held[former, energy, 1]
    l_re, l_im = held[latter, energy, 0], held[latter, energy, 1]
    size = f_re.shape[0]
    f_high, f_low = halves(jnp.concatenate([f_re, f_im], axis=1))
    l_high, l_low = halves(
        jnp.concatenate(
            [jnp.concatenate([l_re, l_im], axis=1), jnp.concatenate([-l_im, l_re], axis=1)], axis=0
        )
    )

    def multiply(one, two):
        return jnp.dot(one, two, preferred_element_type=jnp.float32)

    both = multiply(f_high, l_high) + (multiply(f_high, l_low) + multiply(f_low, l_high))
    held[target, energy, 0] = f_re + l_re + both[:, :size]
    held[target, energy, 1] = f_im + l_im + both[:, size:]


def chain_kernel(
    coupling_low,
    coupling_up,
    lesser,
    greater,
    lesser_full,
    greater_full,
    held,
    full,
    in_sem,
    add_sem,
    out_sem,
    near_send,
    near_recv,
    far_send,
    far_recv,
    relay_send,
):
    energies, _, _, size, _ = lesser.shape
    place = lax.axis_index("seg")
    odd = place % 2
    neighbour = place + 1 - 2 * odd
    across = (place + 2) % 4
    outer = (place == 0) | (place == 3)
    upper = place // 2
    near_side = (1 - upper) * (IDENTITY + place) + upper * (BOTH - place)
    far_side = (1 - upper) * (BOTH - place) + upper * (IDENTITY + place)

    def load(which, segment, energy):
        source = (coupling_low, coupling_up)[which]
        return pltpu.make_async_copy(
            source.at[energy, segment],
            held.at[2 * which + segment, energy],
            in_sem.at[2 * which + segment, energy],
        )

    def load_add(which, segment, energy):
        return pltpu.make_async_copy(
            (lesser, greater)[which].at[energy, segment],
            full.at[which, segment, energy],
            add_sem.at[2 * which + segment, energy],
        )

    def store(which, segment, energy):
        return pltpu.make_async_copy(
            full.at[which, segment, energy],
            (lesser_full, greater_full)[which].at[energy, segment],
            out_sem.at[2 * which + segment, energy],
        )

    def join(segment, energy):
        diagonal = lax.broadcasted_iota(jnp.int32, (size, size), 0) == lax.broadcasted_iota(
            jnp.int32, (size, size), 1
        )
        real_part = held[FIRST + segment, energy, 0] + jnp.where(diagonal, 1.0, 0.0)
        imag_part = held[FIRST + segment, energy, 1]
        for which in (0, 1):
            load_add(which, segment, energy).wait()
        full[0, segment, energy, 0] = full[0, segment, energy, 0] + real_part
        full[0, segment, energy, 1] = full[0, segment, energy, 1] + imag_part
        full[1, segment, energy, 0] = full[1, segment, energy, 0] + real_part
        full[1, segment, energy, 1] = full[1, segment, energy, 1] - imag_part
        for which in (0, 1):
            store(which, segment, energy).start()

    def remote(source, target, send, recv, device):
        return pltpu.make_async_remote_copy(
            src_ref=source,
            dst_ref=target,
            send_sem=send,
            recv_sem=recv,
            device_id={"seg": device},
            device_id_type=MESH,
        )

    def near(energy):
        return remote(
            held.at[LOW_TOTAL + odd, energy],
            held.at[NEAR, energy],
            near_send.at[energy],
            near_recv.at[energy],
            neighbour,
        )

    def far(energy):
        return remote(
            held.at[PAIR, energy], held.at[FAR, energy], far_send.at[energy], far_recv.at[energy], across
        )

    def relay(energy):
        return remote(
            held.at[FAR, energy], held.at[FAR, energy], relay_send.at[energy], far_recv.at[energy], neighbour
        )

    multiply = functools.partial(off_identity_product, held)

    def each(body, count=energies):
        def one(energy, carry):
            body(energy)
            return carry

        lax.fori_loop(0, count, one, 0)

    def load_one(energy):
        for which in (0, 1):
            for segment in (0, 1):
                load(which, segment, energy).start()

    def load_add_one(energy):
        for which in (0, 1):
            for segment in (0, 1):
                load_add(which, segment, energy).start()

    each(load_one)
    each(load_add_one)
    barrier = pltpu.get_barrier_semaphore()
    for device in (neighbour, across):
        pl.semaphore_signal(barrier, inc=1, device_id={"seg": device}, device_id_type=MESH)
    held[IDENTITY] = jnp.zeros(held.shape[1:], jnp.float32)
    pl.semaphore_wait(barrier, 2)

    def totals(turn):
        @pl.when(turn < energies)
        def _():
            for which in (0, 1):
                for segment in (0, 1):
                    load(which, segment, turn).wait()

            multiply(LOW_TOTAL, LOW + 1, LOW, turn)
            multiply(UP_TOTAL, UP, UP + 1, turn)
            near(turn).start()

        @pl.when(turn >= 1)
        def _():
            energy = turn - 1
            near(energy).wait_recv()
            multiply(PAIR, UP_TOTAL - odd, NEAR, energy)

            @pl.when(jnp.logical_not(outer))
            def _():
                far(energy).start()

            multiply(LEFT_ONE + upper, LOW + 3 * upper, near_side, energy)

    each(totals, energies + 1)

    def finish(energy):
        far(energy).wait_recv()

        @pl.when(outer)
        def _():
            relay(energy).start()
            multiply(BOTH, NEAR, FAR, energy)

        multiply(RIGHT_ONE - upper, LOW + 3 * (1 - upper), far_side, energy)
        multiply(FIRST, IDENTITY + place, RIGHT_ONE, energy)
        join(0, energy)
        multiply(SECOND, LEFT_ONE, BOTH - place, energy)
        join(1, energy)

    each(finish)

    def settle(energy):
        near(energy).wait_send()

        @pl.when(outer)
        def _():
            relay(energy).wait_send()

        @pl.when(jnp.logical_not(outer))
        def _():
            far(energy).wait_send()

        for which in (0, 1):
            for segment in (0, 1):
                store(which, segment, energy).wait()

    each(settle)


def chain(coupling_low, coupling_up, lesser, greater):
    energies, segments, _, size, _ = coupling_low.shape
    assert (lax.axis_size("seg"), segments) == (4, 2)
    dma = pltpu.SemaphoreType.DMA
    return pl.pallas_call(
        chain_kernel,
        out_shape=[jax.ShapeDtypeStruct(lesser.shape, jnp.float32)] * 2,
        in_specs=[pl.BlockSpec(memory_space=pl.ANY)] * 4,
        out_specs=[pl.BlockSpec(memory_space=pl.ANY)] * 2,
        scratch_shapes=[
            pltpu.VMEM((SLOTS, energies, 2, size, size), jnp.float32),
            pltpu.VMEM((2, segments, energies, 2, size, size), jnp.float32),
        ]
        + [dma((4, energies))] * 3
        + [dma((energies,))] * 5,
        compiler_params=pltpu.CompilerParams(
            collective_id=1, has_side_effects=True, vmem_limit_bytes=56 * 1024 * 1024
        ),
        cost_estimate=pl.CostEstimate(
            flops=energies * 8 * 3 * 8 * size**3,
            bytes_accessed=energies * segments * 48 * size**2,
            transcendentals=0,
        ),
    )(coupling_low, coupling_up, lesser, greater)


def hand_on_kernel(one, two, one_out, two_out, sem):
    copies = [
        pltpu.make_async_copy(source.at[piece], target.at[piece], sem.at[which, piece])
        for piece in range(one.shape[0])
        for which, (source, target) in enumerate(((one, one_out), (two, two_out)))
    ]
    for copy in copies:
        copy.start()
    for copy in copies:
        copy.wait()


def hand_on(one, two):
    shape = one.shape
    pieces = shape[0] * shape[1]
    flat = (pieces, *shape[2:])
    results = pl.pallas_call(
        hand_on_kernel,
        out_shape=[jax.ShapeDtypeStruct(flat, jnp.float32)] * 2,
        in_specs=[pl.BlockSpec(memory_space=pl.ANY)] * 2,
        out_specs=[pl.BlockSpec(memory_space=pl.ANY)] * 2,
        scratch_shapes=[pltpu.SemaphoreType.DMA((2, pieces))],
        compiler_params=pltpu.CompilerParams(vmem_limit_bytes=16 * 1024 * 1024),
        cost_estimate=pl.CostEstimate(
            flops=0, bytes_accessed=16 * math.prod(shape), transcendentals=0
        ),
    )(one.reshape(flat), two.reshape(flat))
    return tuple(result.reshape(shape) for result in results)


def block_terms(lesser_ref, greater_ref, rows, columns, later):
    size = lesser_ref.shape[0]
    l_re, l_im = lesser_ref[:, 0, rows, columns], lesser_ref[:, 1, rows, columns]
    g_re, g_im = greater_ref[:, 0, rows, columns], greater_ref[:, 1, rows, columns]
    terms = []
    for shift in range(size):
        if later and shift == 0:
            terms.append(None)
            continue
        if later:
            here, there = slice(0, shift), slice(size - shift, size)
        else:
            here, there = slice(shift, size), slice(0, size - shift)
        real_part = l_re[here] * g_re[there] + l_im[here] * g_im[there]
        imag_part = l_im[here] * g_re[there] - l_re[here] * g_im[there]
        terms.append((jnp.sum(real_part, axis=0), jnp.sum(imag_part, axis=0)))
    return terms


def correlate_block(out_ref, pairs, rows, columns, scale):
    total = None
    for lesser_ref, greater_ref, later in pairs:
        terms = block_terms(lesser_ref, greater_ref, rows, columns, later)
        if total is None:
            total = terms
        else:
            total = [
                old if new is None else (old[0] + new[0], old[1] + new[1])
                for old, new in zip(total, terms)
            ]
    for shift, (real_part, imag_part) in enumerate(total):
        out_ref[shift, 0, rows, columns] = real_part * scale
        out_ref[shift, 1, rows, columns] = imag_part * scale


def exchange_kernel(
    scale,
    lesser,
    greater,
    out,
    l_own,
    g_own,
    g_one,
    g_two,
    in_a,
    in_b,
    part,
    own_sem,
    y_send,
    y_recv,
    f_send,
    f_recv,
    o_send,
    o_recv,
    o_own,
):
    chunks, block, _, rows, width = l_own.shape
    share = block // 2
    per_segment = chunks // lesser.shape[1]
    half_rows = lesser.shape[3] // 2
    place = lax.axis_index("energy")
    line = place // 2
    side = place % 2
    partner = place + 1 - 2 * side

    def region(ref, chunk, half):
        start = pl.multiple_of(half * half_rows + (chunk % per_segment) * rows, rows)
        return ref.at[:, chunk // per_segment, :, pl.ds(start, rows), :]

    def remote(source, target, send, recv, device):
        return pltpu.make_async_remote_copy(
            src_ref=source,
            dst_ref=target,
            send_sem=send,
            recv_sem=recv,
            device_id={"energy": device},
            device_id_type=MESH,
        )

    def own_copy(which, chunk):
        source, target = ((lesser, l_own), (greater, g_own))[which]
        return pltpu.make_async_copy(
            region(source, chunk, side),
            target.at[chunk, pl.ds(side * share, share)],
            own_sem.at[which, chunk],
        )

    def side_copy(which, chunk):
        source, target = ((lesser, l_own), (greater, g_own))[which]
        return remote(
            region(source, chunk, 1 - side),
            target.at[chunk, pl.ds(side * share, share)],
            y_send.at[which, chunk],
            y_recv.at[which, chunk],
            partner,
        )

    def issue(chunk):
        for which in (1, 0):
            side_copy(which, chunk).start()
            own_copy(which, chunk).start()

    def ready(which, chunk):
        own_copy(which, chunk).wait()
        side_copy(which, chunk).wait_recv()

    def along(source, target, send, recv, chunk, device):
        return remote(source, target, f_send.at[send, chunk], f_recv.at[recv, chunk], device)

    def arrived(recv, chunk):
        target = (g_one, g_two, in_a, in_b)[recv].at[chunk]
        along(target, target, recv, recv, chunk, partner).wait_recv()

    def result_copy(result, chunk):
        return remote(
            result.at[pl.ds((1 - side) * share, share)],
            region(out, chunk, side),
            o_send.at[chunk],
            o_recv.at[chunk],
            partner,
        )

    def result_own(result, chunk):
        return pltpu.make_async_copy(
            result.at[pl.ds(side * share, share)], region(out, chunk, side), o_own.at[chunk]
        )

    def finish(result, chunk):
        result_copy(result, chunk).start()
        result_own(result, chunk).start()

    def tiles(body):
        columns = width // 128

        def one(index, carry):
            row = pl.multiple_of((index // columns) * 8, 8)
            column = pl.multiple_of((index % columns) * 128, 128)
            body(pl.ds(row, 8), pl.ds(column, 128))
            return carry

        lax.fori_loop(0, (rows // 8) * columns, one, 0)

    def correlate(chunk, *blocks):
        def body(row, column):
            for index, pairs in blocks:
                correlate_block(part.at[chunk, index], pairs, row, column, scale)

        tiles(body)

    def add_in(index, source, chunk):
        part[chunk, index] = part[chunk, index] + source[chunk]

    def sends(chunk):
        def move(source, target, send, recv, device):
            return lambda: along(source, target, send, recv, chunk, device)

        return (
            (move(g_own.at[chunk], g_one.at[chunk], 0, 0, place + 2),),
            (
                move(g_own.at[chunk], g_one.at[chunk], 0, 0, place + 2),
                move(g_one.at[chunk], g_two.at[chunk], 1, 1, place + 2),
                move(part.at[chunk, 0], in_a.at[chunk], 2, 2, place - 2),
            ),
            (
                move(part.at[chunk, 0], in_a.at[chunk], 0, 2, place - 2),
                move(part.at[chunk, 1], in_b.at[chunk], 1, 3, place - 2),
                move(part.at[chunk, 3], in_a.at[chunk], 2, 2, place + 2),
            ),
            (
                move(l_own.at[chunk], in_a.at[chunk], 0, 2, place - 2),
                move(g_own.at[chunk], in_b.at[chunk], 1, 3, place - 2),
            ),
        )

    def result_of(index, chunk):
        return in_a.at[chunk] if index == 3 else part.at[chunk, index]

    def forward(index, chunk):
        l_here, g_here = l_own.at[chunk], g_own.at[chunk]
        one, two = g_one.at[chunk], g_two.at[chunk]
        l_next, g_next = in_a.at[chunk], in_b.at[chunk]
        moves = sends(chunk)[index]
        if index == 0:
            ready(1, chunk)
            moves[0]().start()
            ready(0, chunk)
            correlate(chunk, (0, [(l_here, g_here, False)]))
        elif index == 1:
            ready(1, chunk)
            moves[0]().start()
            arrived(0, chunk)
            moves[1]().start()
            ready(0, chunk)
            correlate(
                chunk,
                (0, [(l_here, g_here, False), (l_here, one, True)]),
                (1, [(l_here, one, False)]),
            )
        elif index == 2:
            ready(1, chunk)
            ready(0, chunk)
            for recv in (2, 3, 0, 1):
                arrived(recv, chunk)
            correlate(
                chunk,
                (
                    0,
                    [
                        (l_here, g_here, False),
                        (l_next, g_next, False),
                        (l_here, one, True),
                        (l_next, g_here, True),
                    ],
                ),
                (
                    1,
                    [
                        (l_here, one, False),
                        (l_next, g_here, False),
                        (l_here, two, True),
                        (l_next, one, True),
                    ],
                ),
                (2, [(l_here, two, False), (l_next, one, False), (l_next, two, True)]),
                (3, [(l_next, two, False)]),
            )
            for move in moves:
                move().start()
            finish(result_of(2, chunk), chunk)
        else:
            ready(0, chunk)
            moves[0]().start()
            ready(1, chunk)
            moves[1]().start()

    def back(index, chunk):
        if index == 0:
            arrived(2, chunk)
            add_in(0, in_a, chunk)
        elif index == 1:
            arrived(2, chunk)
            add_in(0, in_a, chunk)
            sends(chunk)[1][2]().start()
            arrived(3, chunk)
            add_in(1, in_b, chunk)
        elif index == 3:
            arrived(2, chunk)
        if index != 2:
            finish(result_of(index, chunk), chunk)

    barrier = pltpu.get_barrier_semaphore()

    def greet(device):
        pl.semaphore_signal(barrier, inc=1, device_id={"energy": device}, device_id_type=MESH)

    greet(partner)

    @pl.when(line > 0)
    def _():
        greet(place - 2)

    @pl.when(line < 3)
    def _():
        greet(place + 2)

    inner = (line > 0) & (line < 3)

    @pl.when(inner)
    def _():
        pl.semaphore_wait(barrier, 3)

    @pl.when(jnp.logical_not(inner))
    def _():
        pl.semaphore_wait(barrier, 2)

    def start_one(chunk, carry):
        issue(chunk)
        return carry

    lax.fori_loop(0, min(WINDOW, chunks), start_one, 0)

    def role(index):
        lag = LAG + 2 if index == 0 else LAG

        def step(turn, carry):
            @pl.when(turn + WINDOW < chunks)
            def _():
                issue(turn + WINDOW)

            @pl.when(turn < chunks)
            def _():
                forward(index, turn)

            if index != 2:

                @pl.when(turn >= lag)
                def _():
                    back(index, turn - lag)

            return carry

        lax.fori_loop(0, chunks + (0 if index == 2 else lag), step, 0)

        def settle(chunk, carry):
            for which in (0, 1):
                side_copy(which, chunk).wait_send()
            for move in sends(chunk)[index]:
                move().wait_send()
            result = result_of(index, chunk)
            result_own(result, chunk).wait()
            result_copy(result, chunk).wait()
            return carry

        lax.fori_loop(0, chunks, settle, 0)

    for index in range(4):

        @pl.when(line == index)
        def _(index=index):
            role(index)


def correlate_on_line(lesser_full, greater_full):
    share, segments, _, size, width = lesser_full.shape
    chunks = segments * (size // 2) // ROWS
    block = 2 * share
    energies = share * lax.axis_size("energy")
    buffer = pltpu.VMEM((chunks, block, 2, ROWS, width), jnp.float32)
    dma = pltpu.SemaphoreType.DMA
    elements = segments * size * width
    return pl.pallas_call(
        functools.partial(exchange_kernel, 1.0 / math.sqrt(energies)),
        out_shape=jax.ShapeDtypeStruct(lesser_full.shape, jnp.float32),
        in_specs=[pl.BlockSpec(memory_space=pl.ANY)] * 2,
        out_specs=pl.BlockSpec(memory_space=pl.ANY),
        scratch_shapes=[buffer] * 6
        + [pltpu.VMEM((chunks, 4, block, 2, ROWS, width), jnp.float32)]
        + [dma((2, chunks))] * 3
        + [dma((4, chunks))] * 2
        + [dma((chunks,))] * 3,
        compiler_params=pltpu.CompilerParams(
            collective_id=0, has_side_effects=True, vmem_limit_bytes=56 * 1024 * 1024
        ),
        cost_estimate=pl.CostEstimate(
            flops=elements * 400 * 8, bytes_accessed=elements * share * 24, transcendentals=0
        ),
    )(lesser_full, greater_full)


def correlate_rows(lesser_rows, greater_rows):
    energies = lesser_rows.shape[0]
    l_re, l_im = lesser_rows[:, :, 0], lesser_rows[:, :, 1]
    g_re, g_im = greater_rows[:, :, 0], greater_rows[:, :, 1]
    scale = 1.0 / math.sqrt(energies)

    def one(shift, result):
        held = (jnp.arange(energies) + shift < energies)[:, None, None, None]
        s_re = jnp.where(held, jnp.roll(l_re, -shift, axis=0), 0.0)
        s_im = jnp.where(held, jnp.roll(l_im, -shift, axis=0), 0.0)
        real_part = jnp.sum(s_re * g_re + s_im * g_im, axis=0)
        imag_part = jnp.sum(s_im * g_re - s_re * g_im, axis=0)
        row = jnp.stack([real_part, imag_part], axis=1) * scale
        return lax.dynamic_update_index_in_dim(result, row, shift, 0)

    return lax.fori_loop(0, energies, one, jnp.zeros_like(lesser_rows))


def correlate_all(lesser_full, greater_full):
    rows = [
        lax.all_to_all(array, "energy", split_axis=3, concat_axis=0, tiled=True)
        for array in (lesser_full, greater_full)
    ]
    return lax.all_to_all(
        correlate_rows(*rows), "energy", split_axis=0, concat_axis=3, tiled=True
    )


def on_device(lesser, greater, coupling_low, coupling_up):
    lesser_full, greater_full = chain(coupling_low, coupling_up, lesser, greater)
    if lax.axis_size("energy") == 8:
        polarization = correlate_on_line(lesser_full, greater_full)
    else:
        polarization = correlate_all(lesser_full, greater_full)
    return hand_on(polarization, lesser_full)


def solution(mesh):
    spec = P("energy", "seg", None, None, None)
    return jax.shard_map(
        on_device,
        mesh=mesh,
        in_specs=(spec, spec, spec, spec),
        out_specs=(spec, spec),
        check_vma=False,
    )
```

```python
import functools
import math

import jax
import jax.numpy as jnp
from jax import lax
from jax.experimental import pallas as pl
from jax.experimental.pallas import tpu as pltpu
from jax.sharding import PartitionSpec as P

MESH = pl.DeviceIdType.MESH
ROWS = 8
LAG = 6
WINDOW = 2
FLIGHT = 2
AHEAD = (1, 2, 0, 2)


LOW, UP, LOW_TOTAL, UP_TOTAL, PAIR, IDENTITY, NEAR, FAR, BOTH, LEFT_ONE, RIGHT_ONE, FIRST, SECOND = (
    0, 2, 4, 5, 6, 7, 8, 9, 10, 11, 12, 13, 14,
)
SLOTS = 15


def halves(value):
    high = value.astype(jnp.bfloat16)
    return high, (value - high.astype(jnp.float32)).astype(jnp.bfloat16)


def off_identity_product(held, target, former, latter, energy):
    f_re, f_im = held[former, energy, 0], held[former, energy, 1]
    l_re, l_im = held[latter, energy, 0], held[latter, energy, 1]
    size = f_re.shape[0]
    f_high, f_low = halves(jnp.concatenate([f_re, f_im], axis=1))
    l_high, l_low = halves(
        jnp.concatenate(
            [jnp.concatenate([l_re, l_im], axis=1), jnp.concatenate([-l_im, l_re], axis=1)], axis=0
        )
    )

    def multiply(one, two):
        return jnp.dot(one, two, preferred_element_type=jnp.float32)

    both = multiply(f_high, l_high) + (multiply(f_high, l_low) + multiply(f_low, l_high))
    held[target, energy, 0] = f_re + l_re + both[:, :size]
    held[target, energy, 1] = f_im + l_im + both[:, size:]


def chain_kernel(
    coupling_low,
    coupling_up,
    lesser,
    greater,
    lesser_full,
    greater_full,
    held,
    full,
    in_sem,
    add_sem,
    out_sem,
    near_send,
    near_recv,
    far_send,
    far_recv,
    relay_send,
):
    energies, _, _, size, _ = lesser.shape
    place = lax.axis_index("seg")
    odd = place % 2
    neighbour = place + 1 - 2 * odd
    across = (place + 2) % 4
    outer = (place == 0) | (place == 3)
    upper = place // 2
    near_side = (1 - upper) * (IDENTITY + place) + upper * (BOTH - place)
    far_side = (1 - upper) * (BOTH - place) + upper * (IDENTITY + place)

    def load(which, segment, energy):
        source = (coupling_low, coupling_up)[which]
        return pltpu.make_async_copy(
            source.at[energy, segment],
            held.at[2 * which + segment, energy],
            in_sem.at[2 * which + segment, energy],
        )

    def load_add(which, segment, energy):
        return pltpu.make_async_copy(
            (lesser, greater)[which].at[energy, segment],
            full.at[which, segment, energy],
            add_sem.at[2 * which + segment, energy],
        )

    def store(which, segment, energy):
        return pltpu.make_async_copy(
            full.at[which, segment, energy],
            (lesser_full, greater_full)[which].at[energy, segment],
            out_sem.at[2 * which + segment, energy],
        )

    def join(segment, energy):
        diagonal = lax.broadcasted_iota(jnp.int32, (size, size), 0) == lax.broadcasted_iota(
            jnp.int32, (size, size), 1
        )
        real_part = held[FIRST + segment, energy, 0] + jnp.where(diagonal, 1.0, 0.0)
        imag_part = held[FIRST + segment, energy, 1]
        for which in (0, 1):
            load_add(which, segment, energy).wait()
        full[0, segment, energy, 0] = full[0, segment, energy, 0] + real_part
        full[0, segment, energy, 1] = full[0, segment, energy, 1] + imag_part
        full[1, segment, energy, 0] = full[1, segment, energy, 0] + real_part
        full[1, segment, energy, 1] = full[1, segment, energy, 1] - imag_part
        for which in (0, 1):
            store(which, segment, energy).start()

    def remote(source, target, send, recv, device):
        return pltpu.make_async_remote_copy(
            src_ref=source,
            dst_ref=target,
            send_sem=send,
            recv_sem=recv,
            device_id={"seg": device},
            device_id_type=MESH,
        )

    def near(energy):
        return remote(
            held.at[LOW_TOTAL + odd, energy],
            held.at[NEAR, energy],
            near_send.at[energy],
            near_recv.at[energy],
            neighbour,
        )

    def far(energy):
        return remote(
            held.at[PAIR, energy], held.at[FAR, energy], far_send.at[energy], far_recv.at[energy], across
        )

    def relay(energy):
        return remote(
            held.at[FAR, energy], held.at[FAR, energy], relay_send.at[energy], far_recv.at[energy], neighbour
        )

    multiply = functools.partial(off_identity_product, held)

    def each(body, count=energies):
        def one(energy, carry):
            body(energy)
            return carry

        lax.fori_loop(0, count, one, 0)

    def load_one(energy):
        for which in (0, 1):
            for segment in (0, 1):
                load(which, segment, energy).start()

    def load_add_one(energy):
        for which in (0, 1):
            for segment in (0, 1):
                load_add(which, segment, energy).start()

    each(load_one)
    each(load_add_one)
    barrier = pltpu.get_barrier_semaphore()
    for device in (neighbour, across):
        pl.semaphore_signal(barrier, inc=1, device_id={"seg": device}, device_id_type=MESH)
    held[IDENTITY] = jnp.zeros(held.shape[1:], jnp.float32)
    pl.semaphore_wait(barrier, 2)

    def totals(turn):
        @pl.when(turn < energies)
        def _():
            for which in (0, 1):
                for segment in (0, 1):
                    load(which, segment, turn).wait()

            multiply(LOW_TOTAL, LOW + 1, LOW, turn)
            multiply(UP_TOTAL, UP, UP + 1, turn)
            near(turn).start()

        @pl.when(turn >= 1)
        def _():
            energy = turn - 1
            near(energy).wait_recv()
            multiply(PAIR, UP_TOTAL - odd, NEAR, energy)

            @pl.when(jnp.logical_not(outer))
            def _():
                far(energy).start()

            multiply(LEFT_ONE + upper, LOW + 3 * upper, near_side, energy)

    each(totals, energies + 1)

    def finish(energy):
        far(energy).wait_recv()

        @pl.when(outer)
        def _():
            relay(energy).start()
            multiply(BOTH, NEAR, FAR, energy)

        multiply(RIGHT_ONE - upper, LOW + 3 * (1 - upper), far_side, energy)
        multiply(FIRST, IDENTITY + place, RIGHT_ONE, energy)
        join(0, energy)
        multiply(SECOND, LEFT_ONE, BOTH - place, energy)
        join(1, energy)

    each(finish)

    def settle(energy):
        near(energy).wait_send()

        @pl.when(outer)
        def _():
            relay(energy).wait_send()

        @pl.when(jnp.logical_not(outer))
        def _():
            far(energy).wait_send()

        for which in (0, 1):
            for segment in (0, 1):
                store(which, segment, energy).wait()

    each(settle)


def chain(coupling_low, coupling_up, lesser, greater):
    energies, segments, _, size, _ = coupling_low.shape
    assert (lax.axis_size("seg"), segments) == (4, 2)
    dma = pltpu.SemaphoreType.DMA
    return pl.pallas_call(
        chain_kernel,
        out_shape=[jax.ShapeDtypeStruct(lesser.shape, jnp.float32)] * 2,
        in_specs=[pl.BlockSpec(memory_space=pl.ANY)] * 4,
        out_specs=[pl.BlockSpec(memory_space=pl.ANY)] * 2,
        scratch_shapes=[
            pltpu.VMEM((SLOTS, energies, 2, size, size), jnp.float32),
            pltpu.VMEM((2, segments, energies, 2, size, size), jnp.float32),
        ]
        + [dma((4, energies))] * 3
        + [dma((energies,))] * 5,
        compiler_params=pltpu.CompilerParams(
            collective_id=1, has_side_effects=True, vmem_limit_bytes=56 * 1024 * 1024
        ),
        cost_estimate=pl.CostEstimate(
            flops=energies * 8 * 3 * 8 * size**3,
            bytes_accessed=energies * segments * 48 * size**2,
            transcendentals=0,
        ),
    )(coupling_low, coupling_up, lesser, greater)


def hand_on_kernel(one, two, one_out, two_out, sem):
    copies = [
        pltpu.make_async_copy(source.at[piece], target.at[piece], sem.at[which, piece])
        for piece in range(one.shape[0])
        for which, (source, target) in enumerate(((one, one_out), (two, two_out)))
    ]
    for copy in copies:
        copy.start()
    for copy in copies:
        copy.wait()


def hand_on(one, two):
    shape = one.shape
    pieces = shape[0] * shape[1]
    flat = (pieces, *shape[2:])
    results = pl.pallas_call(
        hand_on_kernel,
        out_shape=[jax.ShapeDtypeStruct(flat, jnp.float32)] * 2,
        in_specs=[pl.BlockSpec(memory_space=pl.ANY)] * 2,
        out_specs=[pl.BlockSpec(memory_space=pl.ANY)] * 2,
        scratch_shapes=[pltpu.SemaphoreType.DMA((2, pieces))],
        compiler_params=pltpu.CompilerParams(vmem_limit_bytes=16 * 1024 * 1024),
        cost_estimate=pl.CostEstimate(
            flops=0, bytes_accessed=16 * math.prod(shape), transcendentals=0
        ),
    )(one.reshape(flat), two.reshape(flat))
    return tuple(result.reshape(shape) for result in results)


def block_terms(lesser_ref, greater_ref, rows, columns, later):
    size = lesser_ref.shape[0]
    l_re, l_im = lesser_ref[:, 0, rows, columns], lesser_ref[:, 1, rows, columns]
    g_re, g_im = greater_ref[:, 0, rows, columns], greater_ref[:, 1, rows, columns]
    terms = []
    for shift in range(size):
        if later and shift == 0:
            terms.append(None)
            continue
        if later:
            here, there = slice(0, shift), slice(size - shift, size)
        else:
            here, there = slice(shift, size), slice(0, size - shift)
        real_part = l_re[here] * g_re[there] + l_im[here] * g_im[there]
        imag_part = l_im[here] * g_re[there] - l_re[here] * g_im[there]
        terms.append((jnp.sum(real_part, axis=0), jnp.sum(imag_part, axis=0)))
    return terms


def correlate_block(out_ref, pairs, rows, columns, scale):
    total = None
    for lesser_ref, greater_ref, later in pairs:
        terms = block_terms(lesser_ref, greater_ref, rows, columns, later)
        if total is None:
            total = terms
        else:
            total = [
                old if new is None else (old[0] + new[0], old[1] + new[1])
                for old, new in zip(total, terms)
            ]
    for shift, (real_part, imag_part) in enumerate(total):
        out_ref[shift, 0, rows, columns] = real_part * scale
        out_ref[shift, 1, rows, columns] = imag_part * scale


def exchange_kernel(
    scale,
    lesser,
    greater,
    out,
    l_own,
    g_own,
    g_one,
    g_two,
    in_a,
    in_b,
    part,
    own_sem,
    y_send,
    y_recv,
    f_send,
    f_recv,
    o_send,
    o_recv,
    o_own,
):
    chunks, block, _, rows, width = l_own.shape
    share = block // 2
    per_segment = chunks // lesser.shape[1]
    half_rows = lesser.shape[3] // 2
    place = lax.axis_index("energy")
    line = place // 2
    side = place % 2
    partner = place + 1 - 2 * side

    def region(ref, chunk, half):
        start = pl.multiple_of(half * half_rows + (chunk % per_segment) * rows, rows)
        return ref.at[:, chunk // per_segment, :, pl.ds(start, rows), :]

    def remote(source, target, send, recv, device):
        return pltpu.make_async_remote_copy(
            src_ref=source,
            dst_ref=target,
            send_sem=send,
            recv_sem=recv,
            device_id={"energy": device},
            device_id_type=MESH,
        )

    def own_copy(which, chunk):
        source, target = ((lesser, l_own), (greater, g_own))[which]
        return pltpu.make_async_copy(
            region(source, chunk, side),
            target.at[chunk, pl.ds(side * share, share)],
            own_sem.at[which, chunk],
        )

    def side_copy(which, chunk):
        source, target = ((lesser, l_own), (greater, g_own))[which]
        return remote(
            region(source, chunk, 1 - side),
            target.at[chunk, pl.ds(side * share, share)],
            y_send.at[which, chunk],
            y_recv.at[which, chunk],
            partner,
        )

    def issue(chunk):
        for which in (1, 0):
            side_copy(which, chunk).start()
            own_copy(which, chunk).start()

    def ready(which, chunk):
        own_copy(which, chunk).wait()
        side_copy(which, chunk).wait_recv()

    def along(source, target, send, recv, chunk, device):
        return remote(source, target, f_send.at[send, chunk], f_recv.at[recv, chunk], device)

    def arrived(recv, chunk):
        target = (g_one, g_two, in_a, in_b)[recv].at[chunk]
        along(target, target, recv, recv, chunk, partner).wait_recv()

    def result_copy(result, chunk):
        return remote(
            result.at[pl.ds((1 - side) * share, share)],
            region(out, chunk, side),
            o_send.at[chunk],
            o_recv.at[chunk],
            partner,
        )

    def result_own(result, chunk):
        return pltpu.make_async_copy(
            result.at[pl.ds(side * share, share)], region(out, chunk, side), o_own.at[chunk]
        )

    def finish(result, chunk):
        result_copy(result, chunk).start()
        result_own(result, chunk).start()

    def tiles(body):
        columns = width // 128

        def one(index, carry):
            row = pl.multiple_of((index // columns) * 8, 8)
            column = pl.multiple_of((index % columns) * 128, 128)
            body(pl.ds(row, 8), pl.ds(column, 128))
            return carry

        lax.fori_loop(0, (rows // 8) * columns, one, 0)

    def correlate(chunk, *blocks):
        def body(row, column):
            for index, pairs in blocks:
                correlate_block(part.at[chunk, index], pairs, row, column, scale)

        tiles(body)

    def add_in(index, source, chunk):
        part[chunk, index] = part[chunk, index] + source[chunk]

    def sends(chunk):
        def move(source, target, send, recv, device):
            return lambda: along(source, target, send, recv, chunk, device)

        return (
            (move(g_own.at[chunk], g_one.at[chunk], 0, 0, place + 2),),
            (
                move(g_own.at[chunk], g_one.at[chunk], 0, 0, place + 2),
                move(g_one.at[chunk], g_two.at[chunk], 1, 1, place + 2),
                move(part.at[chunk, 0], in_a.at[chunk], 2, 2, place - 2),
            ),
            (
                move(part.at[chunk, 0], in_a.at[chunk], 0, 2, place - 2),
                move(part.at[chunk, 1], in_b.at[chunk], 1, 3, place - 2),
                move(part.at[chunk, 3], in_a.at[chunk], 2, 2, place + 2),
            ),
            (
                move(l_own.at[chunk], in_a.at[chunk], 0, 2, place - 2),
                move(g_own.at[chunk], in_b.at[chunk], 1, 3, place - 2),
            ),
        )

    def result_of(index, chunk):
        return in_a.at[chunk] if index == 3 else part.at[chunk, index]

    def forward(index, chunk):
        l_here, g_here = l_own.at[chunk], g_own.at[chunk]
        one, two = g_one.at[chunk], g_two.at[chunk]
        l_next, g_next = in_a.at[chunk], in_b.at[chunk]
        moves = sends(chunk)[index]

        @pl.when(chunk >= FLIGHT)
        def _():
            for move in sends(chunk - FLIGHT)[index][: AHEAD[index]]:
                move().wait_send()

        if index == 0:
            ready(1, chunk)
            moves[0]().start()
            ready(0, chunk)
            correlate(chunk, (0, [(l_here, g_here, False)]))
        elif index == 1:
            ready(1, chunk)
            moves[0]().start()
            arrived(0, chunk)
            moves[1]().start()
            ready(0, chunk)
            correlate(
                chunk,
                (0, [(l_here, g_here, False), (l_here, one, True)]),
                (1, [(l_here, one, False)]),
            )
        elif index == 2:
            ready(1, chunk)
            ready(0, chunk)
            for recv in (2, 3, 0, 1):
                arrived(recv, chunk)
            sums = (
                [
                    (l_here, g_here, False),
                    (l_next, g_next, False),
                    (l_here, one, True),
                    (l_next, g_here, True),
                ],
                [
                    (l_here, one, False),
                    (l_next, g_here, False),
                    (l_here, two, True),
                    (l_next, one, True),
                ],
                [(l_here, two, False), (l_next, one, False), (l_next, two, True)],
                [(l_next, two, False)],
            )
            for target, start in ((0, moves[0]), (1, moves[1]), (3, moves[2])):
                correlate(chunk, (target, sums[target]))
                start().start()
            correlate(chunk, (2, sums[2]))
            finish(result_of(2, chunk), chunk)
        else:
            ready(0, chunk)
            moves[0]().start()
            ready(1, chunk)
            moves[1]().start()

    def back(index, chunk):
        if index == 0:
            arrived(2, chunk)
            add_in(0, in_a, chunk)
        elif index == 1:
            arrived(2, chunk)
            add_in(0, in_a, chunk)
            sends(chunk)[1][2]().start()
            arrived(3, chunk)
            add_in(1, in_b, chunk)
        elif index == 3:
            arrived(2, chunk)
        if index != 2:
            finish(result_of(index, chunk), chunk)

    barrier = pltpu.get_barrier_semaphore()

    def greet(device):
        pl.semaphore_signal(barrier, inc=1, device_id={"energy": device}, device_id_type=MESH)

    greet(partner)

    @pl.when(line > 0)
    def _():
        greet(place - 2)

    @pl.when(line < 3)
    def _():
        greet(place + 2)

    inner = (line > 0) & (line < 3)

    @pl.when(inner)
    def _():
        pl.semaphore_wait(barrier, 3)

    @pl.when(jnp.logical_not(inner))
    def _():
        pl.semaphore_wait(barrier, 2)

    def start_one(chunk, carry):
        issue(chunk)
        return carry

    lax.fori_loop(0, min(WINDOW, chunks), start_one, 0)

    def role(index):
        lag = LAG + 2 if index == 0 else LAG

        def step(turn, carry):
            @pl.when(turn + WINDOW < chunks)
            def _():
                issue(turn + WINDOW)

            @pl.when(turn < chunks)
            def _():
                forward(index, turn)

            if index != 2:

                @pl.when(turn >= lag)
                def _():
                    back(index, turn - lag)

            return carry

        lax.fori_loop(0, chunks + (0 if index == 2 else lag), step, 0)

        def settle(chunk, carry):
            for which in (0, 1):
                side_copy(which, chunk).wait_send()
            moves = sends(chunk)[index]
            for move in moves[AHEAD[index] :]:
                move().wait_send()

            @pl.when(chunk >= chunks - FLIGHT)
            def _():
                for move in moves[: AHEAD[index]]:
                    move().wait_send()

            result = result_of(index, chunk)
            result_own(result, chunk).wait()
            result_copy(result, chunk).wait()
            return carry

        lax.fori_loop(0, chunks, settle, 0)

    for index in range(4):

        @pl.when(line == index)
        def _(index=index):
            role(index)


def correlate_on_line(lesser_full, greater_full):
    share, segments, _, size, width = lesser_full.shape
    chunks = segments * (size // 2) // ROWS
    block = 2 * share
    energies = share * lax.axis_size("energy")
    buffer = pltpu.VMEM((chunks, block, 2, ROWS, width), jnp.float32)
    dma = pltpu.SemaphoreType.DMA
    elements = segments * size * width
    return pl.pallas_call(
        functools.partial(exchange_kernel, 1.0 / math.sqrt(energies)),
        out_shape=jax.ShapeDtypeStruct(lesser_full.shape, jnp.float32),
        in_specs=[pl.BlockSpec(memory_space=pl.ANY)] * 2,
        out_specs=pl.BlockSpec(memory_space=pl.ANY),
        scratch_shapes=[buffer] * 6
        + [pltpu.VMEM((chunks, 4, block, 2, ROWS, width), jnp.float32)]
        + [dma((2, chunks))] * 3
        + [dma((4, chunks))] * 2
        + [dma((chunks,))] * 3,
        compiler_params=pltpu.CompilerParams(
            collective_id=0, has_side_effects=True, vmem_limit_bytes=56 * 1024 * 1024
        ),
        cost_estimate=pl.CostEstimate(
            flops=elements * 400 * 8, bytes_accessed=elements * share * 24, transcendentals=0
        ),
    )(lesser_full, greater_full)


def correlate_rows(lesser_rows, greater_rows):
    energies = lesser_rows.shape[0]
    l_re, l_im = lesser_rows[:, :, 0], lesser_rows[:, :, 1]
    g_re, g_im = greater_rows[:, :, 0], greater_rows[:, :, 1]
    scale = 1.0 / math.sqrt(energies)

    def one(shift, result):
        held = (jnp.arange(energies) + shift < energies)[:, None, None, None]
        s_re = jnp.where(held, jnp.roll(l_re, -shift, axis=0), 0.0)
        s_im = jnp.where(held, jnp.roll(l_im, -shift, axis=0), 0.0)
        real_part = jnp.sum(s_re * g_re + s_im * g_im, axis=0)
        imag_part = jnp.sum(s_im * g_re - s_re * g_im, axis=0)
        row = jnp.stack([real_part, imag_part], axis=1) * scale
        return lax.dynamic_update_index_in_dim(result, row, shift, 0)

    return lax.fori_loop(0, energies, one, jnp.zeros_like(lesser_rows))


def correlate_all(lesser_full, greater_full):
    rows = [
        lax.all_to_all(array, "energy", split_axis=3, concat_axis=0, tiled=True)
        for array in (lesser_full, greater_full)
    ]
    return lax.all_to_all(
        correlate_rows(*rows), "energy", split_axis=0, concat_axis=3, tiled=True
    )


def on_device(lesser, greater, coupling_low, coupling_up):
    lesser_full, greater_full = chain(coupling_low, coupling_up, lesser, greater)
    if lax.axis_size("energy") == 8:
        polarization = correlate_on_line(lesser_full, greater_full)
    else:
        polarization = correlate_all(lesser_full, greater_full)
    return hand_on(polarization, lesser_full)


def solution(mesh):
    spec = P("energy", "seg", None, None, None)
    return jax.shard_map(
        on_device,
        mesh=mesh,
        in_specs=(spec, spec, spec, spec),
        out_specs=(spec, spec),
        check_vma=False,
    )
```

```python
import functools
import math

import jax
import jax.numpy as jnp
from jax import lax
from jax.experimental import pallas as pl
from jax.experimental.pallas import tpu as pltpu
from jax.sharding import PartitionSpec as P

MESH = pl.DeviceIdType.MESH
ROWS = 8
COLUMNS = 128
LAG = 10
WINDOW = 4
FLIGHT = 4
AHEAD = (1, 2, 0, 2)


LOW, UP, LOW_TOTAL, UP_TOTAL, PAIR, IDENTITY, NEAR, FAR, BOTH, LEFT_ONE, RIGHT_ONE, FIRST, SECOND = (
    0, 2, 4, 5, 6, 7, 8, 9, 10, 11, 12, 13, 14,
)
SLOTS = 15


def halves(value):
    high = value.astype(jnp.bfloat16)
    return high, (value - high.astype(jnp.float32)).astype(jnp.bfloat16)


def off_identity_product(held, target, former, latter, energy):
    f_re, f_im = held[former, energy, 0], held[former, energy, 1]
    l_re, l_im = held[latter, energy, 0], held[latter, energy, 1]
    size = f_re.shape[0]
    f_high, f_low = halves(jnp.concatenate([f_re, f_im], axis=1))
    l_high, l_low = halves(
        jnp.concatenate(
            [jnp.concatenate([l_re, l_im], axis=1), jnp.concatenate([-l_im, l_re], axis=1)], axis=0
        )
    )

    def multiply(one, two):
        return jnp.dot(one, two, preferred_element_type=jnp.float32)

    both = multiply(f_high, l_high) + (multiply(f_high, l_low) + multiply(f_low, l_high))
    held[target, energy, 0] = f_re + l_re + both[:, :size]
    held[target, energy, 1] = f_im + l_im + both[:, size:]


def chain_kernel(
    coupling_low,
    coupling_up,
    lesser,
    greater,
    lesser_full,
    greater_full,
    held,
    full,
    in_sem,
    add_sem,
    out_sem,
    near_send,
    near_recv,
    far_send,
    far_recv,
    relay_send,
):
    energies, _, _, size, _ = lesser.shape
    place = lax.axis_index("seg")
    odd = place % 2
    neighbour = place + 1 - 2 * odd
    across = (place + 2) % 4
    outer = (place == 0) | (place == 3)
    upper = place // 2
    near_side = (1 - upper) * (IDENTITY + place) + upper * (BOTH - place)
    far_side = (1 - upper) * (BOTH - place) + upper * (IDENTITY + place)

    def load(which, segment, energy):
        source = (coupling_low, coupling_up)[which]
        return pltpu.make_async_copy(
            source.at[energy, segment],
            held.at[2 * which + segment, energy],
            in_sem.at[2 * which + segment, energy],
        )

    def load_add(which, segment, energy):
        return pltpu.make_async_copy(
            (lesser, greater)[which].at[energy, segment],
            full.at[which, segment, energy],
            add_sem.at[2 * which + segment, energy],
        )

    def store(which, segment, energy):
        return pltpu.make_async_copy(
            full.at[which, segment, energy],
            (lesser_full, greater_full)[which].at[energy, segment],
            out_sem.at[2 * which + segment, energy],
        )

    def join(segment, energy):
        diagonal = lax.broadcasted_iota(jnp.int32, (size, size), 0) == lax.broadcasted_iota(
            jnp.int32, (size, size), 1
        )
        real_part = held[FIRST + segment, energy, 0] + jnp.where(diagonal, 1.0, 0.0)
        imag_part = held[FIRST + segment, energy, 1]
        for which in (0, 1):
            load_add(which, segment, energy).wait()
        full[0, segment, energy, 0] = full[0, segment, energy, 0] + real_part
        full[0, segment, energy, 1] = full[0, segment, energy, 1] + imag_part
        full[1, segment, energy, 0] = full[1, segment, energy, 0] + real_part
        full[1, segment, energy, 1] = full[1, segment, energy, 1] - imag_part
        for which in (0, 1):
            store(which, segment, energy).start()

    def remote(source, target, send, recv, device):
        return pltpu.make_async_remote_copy(
            src_ref=source,
            dst_ref=target,
            send_sem=send,
            recv_sem=recv,
            device_id={"seg": device},
            device_id_type=MESH,
        )

    def near(energy):
        return remote(
            held.at[LOW_TOTAL + odd, energy],
            held.at[NEAR, energy],
            near_send.at[energy],
            near_recv.at[energy],
            neighbour,
        )

    def far(energy):
        return remote(
            held.at[PAIR, energy], held.at[FAR, energy], far_send.at[energy], far_recv.at[energy], across
        )

    def relay(energy):
        return remote(
            held.at[FAR, energy], held.at[FAR, energy], relay_send.at[energy], far_recv.at[energy], neighbour
        )

    multiply = functools.partial(off_identity_product, held)

    def each(body, count=energies):
        def one(energy, carry):
            body(energy)
            return carry

        lax.fori_loop(0, count, one, 0)

    def load_one(energy):
        for which in (0, 1):
            for segment in (0, 1):
                load(which, segment, energy).start()

    def load_add_one(energy):
        for which in (0, 1):
            for segment in (0, 1):
                load_add(which, segment, energy).start()

    each(load_one)
    each(load_add_one)
    barrier = pltpu.get_barrier_semaphore()
    for device in (neighbour, across):
        pl.semaphore_signal(barrier, inc=1, device_id={"seg": device}, device_id_type=MESH)
    held[IDENTITY] = jnp.zeros(held.shape[1:], jnp.float32)
    pl.semaphore_wait(barrier, 2)

    def totals(turn):
        @pl.when(turn < energies)
        def _():
            for which in (0, 1):
                for segment in (0, 1):
                    load(which, segment, turn).wait()

            multiply(LOW_TOTAL, LOW + 1, LOW, turn)
            multiply(UP_TOTAL, UP, UP + 1, turn)
            near(turn).start()

        @pl.when(turn >= 1)
        def _():
            energy = turn - 1
            near(energy).wait_recv()
            multiply(PAIR, UP_TOTAL - odd, NEAR, energy)

            @pl.when(jnp.logical_not(outer))
            def _():
                far(energy).start()

            multiply(LEFT_ONE + upper, LOW + 3 * upper, near_side, energy)

    each(totals, energies + 1)

    def finish(energy):
        far(energy).wait_recv()

        @pl.when(outer)
        def _():
            relay(energy).start()
            multiply(BOTH, NEAR, FAR, energy)

        multiply(RIGHT_ONE - upper, LOW + 3 * (1 - upper), far_side, energy)
        multiply(FIRST, IDENTITY + place, RIGHT_ONE, energy)
        join(0, energy)
        multiply(SECOND, LEFT_ONE, BOTH - place, energy)
        join(1, energy)

    each(finish)

    def settle(energy):
        near(energy).wait_send()

        @pl.when(outer)
        def _():
            relay(energy).wait_send()

        @pl.when(jnp.logical_not(outer))
        def _():
            far(energy).wait_send()

        for which in (0, 1):
            for segment in (0, 1):
                store(which, segment, energy).wait()

    each(settle)


def chain(coupling_low, coupling_up, lesser, greater):
    energies, segments, _, size, _ = coupling_low.shape
    assert (lax.axis_size("seg"), segments) == (4, 2)
    dma = pltpu.SemaphoreType.DMA
    return pl.pallas_call(
        chain_kernel,
        out_shape=[jax.ShapeDtypeStruct(lesser.shape, jnp.float32)] * 2,
        in_specs=[pl.BlockSpec(memory_space=pl.ANY)] * 4,
        out_specs=[pl.BlockSpec(memory_space=pl.ANY)] * 2,
        scratch_shapes=[
            pltpu.VMEM((SLOTS, energies, 2, size, size), jnp.float32),
            pltpu.VMEM((2, segments, energies, 2, size, size), jnp.float32),
        ]
        + [dma((4, energies))] * 3
        + [dma((energies,))] * 5,
        compiler_params=pltpu.CompilerParams(
            collective_id=1, has_side_effects=True, vmem_limit_bytes=56 * 1024 * 1024
        ),
        cost_estimate=pl.CostEstimate(
            flops=energies * 8 * 3 * 8 * size**3,
            bytes_accessed=energies * segments * 48 * size**2,
            transcendentals=0,
        ),
    )(coupling_low, coupling_up, lesser, greater)


def hand_on_kernel(one, two, one_out, two_out, sem):
    copies = [
        pltpu.make_async_copy(source.at[piece], target.at[piece], sem.at[which, piece])
        for piece in range(one.shape[0])
        for which, (source, target) in enumerate(((one, one_out), (two, two_out)))
    ]
    for copy in copies:
        copy.start()
    for copy in copies:
        copy.wait()


def hand_on(one, two):
    shape = one.shape
    pieces = shape[0] * shape[1]
    flat = (pieces, *shape[2:])
    results = pl.pallas_call(
        hand_on_kernel,
        out_shape=[jax.ShapeDtypeStruct(flat, jnp.float32)] * 2,
        in_specs=[pl.BlockSpec(memory_space=pl.ANY)] * 2,
        out_specs=[pl.BlockSpec(memory_space=pl.ANY)] * 2,
        scratch_shapes=[pltpu.SemaphoreType.DMA((2, pieces))],
        compiler_params=pltpu.CompilerParams(vmem_limit_bytes=16 * 1024 * 1024),
        cost_estimate=pl.CostEstimate(
            flops=0, bytes_accessed=16 * math.prod(shape), transcendentals=0
        ),
    )(one.reshape(flat), two.reshape(flat))
    return tuple(result.reshape(shape) for result in results)


def block_terms(lesser_ref, greater_ref, rows, columns, later):
    size = lesser_ref.shape[0]
    l_re, l_im = lesser_ref[:, 0, rows, columns], lesser_ref[:, 1, rows, columns]
    g_re, g_im = greater_ref[:, 0, rows, columns], greater_ref[:, 1, rows, columns]
    terms = []
    for shift in range(size):
        if later and shift == 0:
            terms.append(None)
            continue
        if later:
            here, there = slice(0, shift), slice(size - shift, size)
        else:
            here, there = slice(shift, size), slice(0, size - shift)
        real_part = l_re[here] * g_re[there] + l_im[here] * g_im[there]
        imag_part = l_im[here] * g_re[there] - l_re[here] * g_im[there]
        terms.append((jnp.sum(real_part, axis=0), jnp.sum(imag_part, axis=0)))
    return terms


def correlate_block(out_ref, pairs, rows, columns, scale):
    total = None
    for lesser_ref, greater_ref, later in pairs:
        terms = block_terms(lesser_ref, greater_ref, rows, columns, later)
        if total is None:
            total = terms
        else:
            total = [
                old if new is None else (old[0] + new[0], old[1] + new[1])
                for old, new in zip(total, terms)
            ]
    for shift, (real_part, imag_part) in enumerate(total):
        out_ref[shift, 0, rows, columns] = real_part * scale
        out_ref[shift, 1, rows, columns] = imag_part * scale


def exchange_kernel(
    scale,
    lesser,
    greater,
    out,
    l_own,
    g_own,
    g_one,
    g_two,
    in_a,
    in_b,
    part,
    own_sem,
    y_send,
    y_recv,
    f_send,
    f_recv,
    o_send,
    o_recv,
    o_own,
):
    chunks, block, _, rows, width = l_own.shape
    share = block // 2
    per_segment = chunks // lesser.shape[1]
    half_rows = lesser.shape[3] // 2
    across = lesser.shape[4] // width
    place = lax.axis_index("energy")
    line = place // 2
    side = place % 2
    partner = place + 1 - 2 * side

    def region(ref, chunk, half):
        within = chunk % per_segment
        row = pl.multiple_of(half * half_rows + (within // across) * rows, rows)
        column = pl.multiple_of((within % across) * width, width)
        return ref.at[:, chunk // per_segment, :, pl.ds(row, rows), pl.ds(column, width)]

    def remote(source, target, send, recv, device):
        return pltpu.make_async_remote_copy(
            src_ref=source,
            dst_ref=target,
            send_sem=send,
            recv_sem=recv,
            device_id={"energy": device},
            device_id_type=MESH,
        )

    def own_copy(which, chunk):
        source, target = ((lesser, l_own), (greater, g_own))[which]
        return pltpu.make_async_copy(
            region(source, chunk, side),
            target.at[chunk, pl.ds(side * share, share)],
            own_sem.at[which, chunk],
        )

    def side_copy(which, chunk):
        source, target = ((lesser, l_own), (greater, g_own))[which]
        return remote(
            region(source, chunk, 1 - side),
            target.at[chunk, pl.ds(side * share, share)],
            y_send.at[which, chunk],
            y_recv.at[which, chunk],
            partner,
        )

    def issue(chunk):
        for which in (1, 0):
            side_copy(which, chunk).start()
            own_copy(which, chunk).start()

    def ready(which, chunk):
        own_copy(which, chunk).wait()
        side_copy(which, chunk).wait_recv()

    def along(source, target, send, recv, chunk, device):
        return remote(source, target, f_send.at[send, chunk], f_recv.at[recv, chunk], device)

    def arrived(recv, chunk):
        target = (g_one, g_two, in_a, in_b)[recv].at[chunk]
        along(target, target, recv, recv, chunk, partner).wait_recv()

    def result_copy(result, chunk):
        return remote(
            result.at[pl.ds((1 - side) * share, share)],
            region(out, chunk, side),
            o_send.at[chunk],
            o_recv.at[chunk],
            partner,
        )

    def result_own(result, chunk):
        return pltpu.make_async_copy(
            result.at[pl.ds(side * share, share)], region(out, chunk, side), o_own.at[chunk]
        )

    def finish(result, chunk):
        result_copy(result, chunk).start()
        result_own(result, chunk).start()

    def tiles(body):
        columns = width // 128

        def one(index, carry):
            row = pl.multiple_of((index // columns) * 8, 8)
            column = pl.multiple_of((index % columns) * 128, 128)
            body(pl.ds(row, 8), pl.ds(column, 128))
            return carry

        lax.fori_loop(0, (rows // 8) * columns, one, 0)

    def correlate(chunk, *blocks):
        def body(row, column):
            for index, pairs in blocks:
                correlate_block(part.at[chunk, index], pairs, row, column, scale)

        tiles(body)

    def add_in(index, source, chunk):
        part[chunk, index] = part[chunk, index] + source[chunk]

    def sends(chunk):
        def move(source, target, send, recv, device):
            return lambda: along(source, target, send, recv, chunk, device)

        return (
            (move(g_own.at[chunk], g_one.at[chunk], 0, 0, place + 2),),
            (
                move(g_own.at[chunk], g_one.at[chunk], 0, 0, place + 2),
                move(g_one.at[chunk], g_two.at[chunk], 1, 1, place + 2),
                move(part.at[chunk, 0], in_a.at[chunk], 2, 2, place - 2),
            ),
            (
                move(part.at[chunk, 0], in_a.at[chunk], 0, 2, place - 2),
                move(part.at[chunk, 1], in_b.at[chunk], 1, 3, place - 2),
                move(part.at[chunk, 3], in_a.at[chunk], 2, 2, place + 2),
            ),
            (
                move(l_own.at[chunk], in_a.at[chunk], 0, 2, place - 2),
                move(g_own.at[chunk], in_b.at[chunk], 1, 3, place - 2),
            ),
        )

    def result_of(index, chunk):
        return in_a.at[chunk] if index == 3 else part.at[chunk, index]

    def forward(index, chunk):
        l_here, g_here = l_own.at[chunk], g_own.at[chunk]
        one, two = g_one.at[chunk], g_two.at[chunk]
        l_next, g_next = in_a.at[chunk], in_b.at[chunk]
        moves = sends(chunk)[index]

        @pl.when(chunk >= FLIGHT)
        def _():
            for move in sends(chunk - FLIGHT)[index][: AHEAD[index]]:
                move().wait_send()

        if index == 0:
            ready(1, chunk)
            moves[0]().start()
            ready(0, chunk)
            correlate(chunk, (0, [(l_here, g_here, False)]))
        elif index == 1:
            ready(1, chunk)
            moves[0]().start()
            arrived(0, chunk)
            moves[1]().start()
            ready(0, chunk)
            correlate(
                chunk,
                (0, [(l_here, g_here, False), (l_here, one, True)]),
                (1, [(l_here, one, False)]),
            )
        elif index == 2:
            ready(1, chunk)
            ready(0, chunk)
            for recv in (2, 3, 0, 1):
                arrived(recv, chunk)
            sums = (
                [
                    (l_here, g_here, False),
                    (l_next, g_next, False),
                    (l_here, one, True),
                    (l_next, g_here, True),
                ],
                [
                    (l_here, one, False),
                    (l_next, g_here, False),
                    (l_here, two, True),
                    (l_next, one, True),
                ],
                [(l_here, two, False), (l_next, one, False), (l_next, two, True)],
                [(l_next, two, False)],
            )
            for target, start in ((0, moves[0]), (1, moves[1]), (3, moves[2])):
                correlate(chunk, (target, sums[target]))
                start().start()
            correlate(chunk, (2, sums[2]))
            finish(result_of(2, chunk), chunk)
        else:
            ready(0, chunk)
            moves[0]().start()
            ready(1, chunk)
            moves[1]().start()

    def back(index, chunk):
        if index == 0:
            arrived(2, chunk)
            add_in(0, in_a, chunk)
        elif index == 1:
            arrived(2, chunk)
            add_in(0, in_a, chunk)
            sends(chunk)[1][2]().start()
            arrived(3, chunk)
            add_in(1, in_b, chunk)
        elif index == 3:
            arrived(2, chunk)
        if index != 2:
            finish(result_of(index, chunk), chunk)

    barrier = pltpu.get_barrier_semaphore()

    def greet(device):
        pl.semaphore_signal(barrier, inc=1, device_id={"energy": device}, device_id_type=MESH)

    greet(partner)

    @pl.when(line > 0)
    def _():
        greet(place - 2)

    @pl.when(line < 3)
    def _():
        greet(place + 2)

    inner = (line > 0) & (line < 3)

    @pl.when(inner)
    def _():
        pl.semaphore_wait(barrier, 3)

    @pl.when(jnp.logical_not(inner))
    def _():
        pl.semaphore_wait(barrier, 2)

    def start_one(chunk, carry):
        issue(chunk)
        return carry

    lax.fori_loop(0, min(WINDOW, chunks), start_one, 0)

    def role(index):
        lag = LAG + 2 if index == 0 else LAG

        def step(turn, carry):
            @pl.when(turn + WINDOW < chunks)
            def _():
                issue(turn + WINDOW)

            @pl.when(turn < chunks)
            def _():
                forward(index, turn)

            if index != 2:

                @pl.when(turn >= lag)
                def _():
                    back(index, turn - lag)

            return carry

        lax.fori_loop(0, chunks + (0 if index == 2 else lag), step, 0)

        def settle(chunk, carry):
            for which in (0, 1):
                side_copy(which, chunk).wait_send()
            moves = sends(chunk)[index]
            for move in moves[AHEAD[index] :]:
                move().wait_send()

            @pl.when(chunk >= chunks - FLIGHT)
            def _():
                for move in moves[: AHEAD[index]]:
                    move().wait_send()

            result = result_of(index, chunk)
            result_own(result, chunk).wait()
            result_copy(result, chunk).wait()
            return carry

        lax.fori_loop(0, chunks, settle, 0)

    for index in range(4):

        @pl.when(line == index)
        def _(index=index):
            role(index)


def correlate_on_line(lesser_full, greater_full):
    share, segments, _, size, width = lesser_full.shape
    chunks = segments * (size // 2 // ROWS) * (width // COLUMNS)
    block = 2 * share
    energies = share * lax.axis_size("energy")
    buffer = pltpu.VMEM((chunks, block, 2, ROWS, COLUMNS), jnp.float32)
    dma = pltpu.SemaphoreType.DMA
    elements = segments * size * width
    return pl.pallas_call(
        functools.partial(exchange_kernel, 1.0 / math.sqrt(energies)),
        out_shape=jax.ShapeDtypeStruct(lesser_full.shape, jnp.float32),
        in_specs=[pl.BlockSpec(memory_space=pl.ANY)] * 2,
        out_specs=pl.BlockSpec(memory_space=pl.ANY),
        scratch_shapes=[buffer] * 6
        + [pltpu.VMEM((chunks, 4, block, 2, ROWS, COLUMNS), jnp.float32)]
        + [dma((2, chunks))] * 3
        + [dma((4, chunks))] * 2
        + [dma((chunks,))] * 3,
        compiler_params=pltpu.CompilerParams(
            collective_id=0, has_side_effects=True, vmem_limit_bytes=56 * 1024 * 1024
        ),
        cost_estimate=pl.CostEstimate(
            flops=elements * 400 * 8, bytes_accessed=elements * share * 24, transcendentals=0
        ),
    )(lesser_full, greater_full)


def correlate_rows(lesser_rows, greater_rows):
    energies = lesser_rows.shape[0]
    l_re, l_im = lesser_rows[:, :, 0], lesser_rows[:, :, 1]
    g_re, g_im = greater_rows[:, :, 0], greater_rows[:, :, 1]
    scale = 1.0 / math.sqrt(energies)

    def one(shift, result):
        held = (jnp.arange(energies) + shift < energies)[:, None, None, None]
        s_re = jnp.where(held, jnp.roll(l_re, -shift, axis=0), 0.0)
        s_im = jnp.where(held, jnp.roll(l_im, -shift, axis=0), 0.0)
        real_part = jnp.sum(s_re * g_re + s_im * g_im, axis=0)
        imag_part = jnp.sum(s_im * g_re - s_re * g_im, axis=0)
        row = jnp.stack([real_part, imag_part], axis=1) * scale
        return lax.dynamic_update_index_in_dim(result, row, shift, 0)

    return lax.fori_loop(0, energies, one, jnp.zeros_like(lesser_rows))


def correlate_all(lesser_full, greater_full):
    rows = [
        lax.all_to_all(array, "energy", split_axis=3, concat_axis=0, tiled=True)
        for array in (lesser_full, greater_full)
    ]
    return lax.all_to_all(
        correlate_rows(*rows), "energy", split_axis=0, concat_axis=3, tiled=True
    )


def on_device(lesser, greater, coupling_low, coupling_up):
    lesser_full, greater_full = chain(coupling_low, coupling_up, lesser, greater)
    if lax.axis_size("energy") == 8:
        polarization = correlate_on_line(lesser_full, greater_full)
    else:
        polarization = correlate_all(lesser_full, greater_full)
    return hand_on(polarization, lesser_full)


def solution(mesh):
    spec = P("energy", "seg", None, None, None)
    return jax.shard_map(
        on_device,
        mesh=mesh,
        in_specs=(spec, spec, spec, spec),
        out_specs=(spec, spec),
        check_vma=False,
    )
```
